128 devices in a mesh: seq: 16 (over y, z), head: 8 (over x, core).
Axes of the slice: x: 4, y: 4, z: 4, core: 2. Of those that a mesh axis runs over, the one named last changes fastest.
Arguments:
- queries: bfloat16 [16384, 4096], P('seq', 'head'), may hold values from -6 to 6
- keys: bfloat16 [16384, 4096], P('seq', 'head'), may hold values from -6 to 6
- values: bfloat16 [16384, 4096], P('seq', 'head'), may hold values from -6 to 6
- decay: float32 [16384, 4096], P('seq', 'head'), as said below
- beta: float32 [32, 16384], P('head', 'seq'), may hold values from 0.002 to 0.98
- wy_inverse: float32 [256, 64, 2048], P('seq', None, 'head')
- out_gate: bfloat16 [16384, 4096], P('seq', 'head'), may hold values from -6 to 6
- norm_gain: float32 [128], replicated, may hold values from 0.1 to 1.9
- out_proj: bfloat16 [4096, 2304], P('head'), may hold values from -0.125 to 0.125
- grad_out: bfloat16 [16384, 2304], P('seq', 'head'), may hold values from -6 to 6
- resets: int32 [16], P('seq'), may hold values from 0 to 16, as said below
Outputs:
- grad_queries: bfloat16 [16384, 4096], P('seq', 'head')
- grad_keys: bfloat16 [16384, 4096], P('seq', 'head')
- grad_values: bfloat16 [16384, 4096], P('seq', 'head')
- grad_decay: float32 [16384, 4096], P('seq', 'head')
- grad_beta: float32 [32, 16384], P('head', 'seq')
- grad_gate: bfloat16 [16384, 4096], P('seq', 'head')
The draws below stay inside these ranges and needn't reach their ends.
Inputs may be any that keep to these rules, and one draw needn't show every extreme that they name: `resets`: 16 means that no document starts in that index of seq; the first value is 0 and the last is 16. Natural logarithms of decay factors, at most 0.
All inputs are finite; a program needn't handle non-finite values.
Results may differ from the reference program's by a relative error of at most 0.02.
Values may be sent and summed in bfloat16 or wider, within the bound.
No kernel may reach another device: no remote copies, remote signals or barrier semaphores. Data moves between devices by JAX's collectives and lax.ppermute only.
A program may use at most 192 MiB of HBM per device.

```python
import math
import jax
import jax.numpy as jnp
from jax import lax

H = 32
DK = 128
DV = 128
D = 2304
GROUP = 64
TOK_DEV = 1024
TOKENS = 16384
CH_DEV = 16


def shared_fields(key, slow_share):
    key_keys = jax.random.fold_in(key, 101)
    key_decay = jax.random.fold_in(key, 102)
    key_beta = jax.random.fold_in(key, 103)
    columns = H * DK
    keys_f = jnp.clip(jax.random.normal(key_keys, (TOKENS, columns)), -6.0, 6.0)
    keys_f = keys_f.astype(jnp.bfloat16).astype(jnp.float32)
    parts = jax.random.split(key_decay, 7)
    slow = jax.random.uniform(parts[0], (columns,)) < slow_share
    slow_rate = jnp.exp(jax.random.uniform(parts[1], (columns,), minval=math.log(0.02 / TOKENS), maxval=math.log(0.2 / TOKENS)))
    fast_rate = jax.random.uniform(parts[2], (columns,), minval=1.0 / 50.0, maxval=1.0 / 30.0)
    baseline_level = jnp.where(slow, slow_rate, fast_rate)
    coarse_estimate = jax.random.uniform(parts[3], (TOKENS, columns), minval=0.5, maxval=1.5)
    blocks_count = TOKENS // TOK_DEV
    multiplier_term = jnp.exp(jax.random.uniform(parts[4], (blocks_count,), minval=math.log(0.5), maxval=math.log(2.0)))
    multiplier_term = jnp.repeat(multiplier_term, TOK_DEV)[:, None]
    reset_locations = jax.random.randint(parts[5], (2,), 0, TOKENS)
    loss_values = jnp.log(jax.random.uniform(parts[6], (2,), minval=0.6, maxval=0.8))
    token_positions = jnp.arange(TOKENS)[:, None]
    spike_amount = jnp.sum(jnp.where(token_positions == reset_locations[None, :], loss_values[None, :], 0.0), axis=1)[:, None]
    decay = (-baseline_level[None, :] * coarse_estimate * multiplier_term + spike_amount).astype(jnp.float32)
    beta_keys = jax.random.split(key_beta, 3)
    quiet = jax.random.uniform(beta_keys[0], (H,)) < 0.5
    center = jnp.where(quiet, -5.5, jax.random.uniform(beta_keys[1], (H,), minval=-1.0, maxval=1.5))
    spread = jnp.where(quiet, 1.0, 1.5)
    noise = jax.random.normal(beta_keys[2], (H, TOKENS))
    beta = jnp.clip(jax.nn.sigmoid(center[:, None] + spread[:, None] * noise), 0.002, 0.98)
    return (keys_f, decay, beta.astype(jnp.float32))


def block_inverse(keys_f, decay, beta):
    count = TOKENS // GROUP
    rows = keys_f.reshape(TOKENS, H, DK)
    unit = rows * lax.rsqrt(jnp.sum(rows * rows, axis=-1, keepdims=True) + 1e-06)
    unit = unit.reshape(count, GROUP, H, DK).transpose(0, 2, 1, 3)
    gates = decay.reshape(count, GROUP, H, DK).transpose(0, 2, 1, 3)
    cumul = jnp.cumsum(gates, axis=2)
    key_dec = unit * jnp.exp(cumul)
    key_inv = unit * jnp.exp(-cumul)
    strength = beta.reshape(H, count, GROUP).transpose(1, 0, 2)
    strict = jnp.einsum('chid,chjd->chij', key_dec, key_inv, precision=lax.Precision.HIGHEST)
    strict = strict * strength[:, :, :, None]
    below = (jnp.arange(GROUP)[None, :] < jnp.arange(GROUP)[:, None]).astype(jnp.float32)
    strict = strict * below
    eye = jnp.eye(GROUP, dtype=jnp.float32)
    start = jnp.broadcast_to(eye, strict.shape)

    def solve_row(index, result):
        coeffs = lax.dynamic_index_in_dim(strict, index, 2, keepdims=False)
        row = lax.dynamic_index_in_dim(eye, index, 0, keepdims=False)
        row = row - jnp.einsum('chj,chjk->chk', coeffs, result, precision=lax.Precision.HIGHEST)
        return lax.dynamic_update_index_in_dim(result, row, index, 2)
    inverse = lax.fori_loop(0, GROUP, solve_row, start)
    return inverse.transpose(0, 2, 1, 3).reshape(count, GROUP, H * GROUP).astype(jnp.float32)


def draw_keys(key, part):
    fields = shared_fields(key, 0.5)
    return fields[0].astype(jnp.bfloat16)


def draw_beta(key, part):
    fields = shared_fields(key, 0.5)
    return fields[2].astype(jnp.float32)


def draw_decay(key, part):
    fields = shared_fields(key, 0.5)
    return fields[1].astype(jnp.float32)


def draw_wy_inverse(key, part):
    fields = shared_fields(key, 0.5)
    return block_inverse(fields[0], fields[1], fields[2])


def draw_resets(key, part):
    key = jax.random.fold_in(key, 11)
    blocks_count = TOKENS // TOK_DEV
    drawn_starts = jax.random.randint(key, (blocks_count,), 0, 4 * CH_DEV)
    chosen = jnp.where(drawn_starts < CH_DEV, drawn_starts, CH_DEV)
    reset_locations = jnp.arange(blocks_count)
    chosen = jnp.where(reset_locations == 0, 0, jnp.where(reset_locations == blocks_count - 1, CH_DEV, chosen))
    return chosen.astype(jnp.int32)


def levels(rng, extent, shards, smallest, largest):
    factor_of = 1.0
    for position, blocks in shards:
        heights = jax.random.uniform(jax.random.fold_in(jax.random.fold_in(rng, 6), position), (blocks,), jnp.float32, smallest / len(shards), largest / len(shards))
        factor_of = factor_of * jnp.repeat(jnp.exp(heights), extent[position] // blocks).reshape((-1,) + (1,) * (len(extent) - 1 - position))
    return factor_of


def scatter_about(own_key, dims, scale, bound, shards=(), kind=jnp.bfloat16):
    level = levels(own_key, dims, shards, -0.22, 0.18) if shards else 1.0
    values = jax.random.normal(own_key, dims, jnp.float32) * scale * level
    return jnp.minimum(jnp.maximum(values, -bound), bound).astype(kind)


def setup_inputs(seed: int = 0) -> dict:
    arg_keys = jax.random.split(jax.random.key(seed), 12)
    return {
        "queries": scatter_about(arg_keys[0], (TOKENS, H * DK), 1.0, 6.0, ((0, 16), (1, 8))),
        "keys": draw_keys(jax.random.fold_in(arg_keys[11], 71), 0),
        "values": scatter_about(arg_keys[2], (TOKENS, H * DV), 1.0, 6.0, ((0, 16), (1, 8))),
        "decay": draw_decay(jax.random.fold_in(arg_keys[11], 71), 0),
        "beta": draw_beta(jax.random.fold_in(arg_keys[11], 71), 0),
        "wy_inverse": draw_wy_inverse(jax.random.fold_in(arg_keys[11], 71), 0),
        "out_gate": scatter_about(arg_keys[6], (TOKENS, H * DV), 1.0, 6.0, ((0, 16), (1, 8))),
        "norm_gain": jnp.clip(1.0 + 0.18 * jax.random.normal(arg_keys[7], (DV,), jnp.float32), 0.1, 1.9),
        "out_proj": scatter_about(arg_keys[8], (H * DV, D), D ** -0.5, 0.125, ((0, 8),)),
        "grad_out": scatter_about(arg_keys[9], (TOKENS, D), 1.0, 6.0, ((0, 16), (1, 8))),
        "resets": draw_resets(jax.random.fold_in(arg_keys[11], 71), 0),
    }


precise = lax.Precision.HIGHEST

def to_blocks(array, heads, width):
    count = array.shape[0] // GROUP
    return array.reshape(count, GROUP, heads, width).transpose(0, 2, 1, 3)

def from_blocks(array):
    count, heads, length, width = array.shape
    return array.transpose(0, 2, 1, 3).reshape(count * length, heads * width)

def unit_rows(array, width, multiplier_term):
    rows = array.reshape(array.shape[0], -1, width)
    scale = lax.rsqrt(lax.optimization_barrier(jnp.sum(rows * rows, axis=-1, keepdims=True)) + 1e-06)
    return (rows * scale * multiplier_term).reshape(array.shape)

def low_product(form, left, right):
    return jnp.einsum(form, left.astype(jnp.bfloat16), right.astype(jnp.bfloat16), preferred_element_type=jnp.float32)

def group_step(state, block):
    query_rows, key_rows, value_rows, gate_rows, beta_rows, wy_rows, keep_flag = block
    entry = state * keep_flag
    cumul = jnp.cumsum(gate_rows, axis=1)
    final = cumul[:, -1:, :]
    query_dec = query_rows * jnp.exp(cumul)
    key_dec = key_rows * jnp.exp(cumul)
    key_inv = key_rows * jnp.exp(-cumul)
    key_tail = key_rows * jnp.exp(final - cumul)
    lower = jnp.tril(jnp.ones((GROUP, GROUP), jnp.float32))
    predicted = jnp.einsum('hld,hdv->hlv', key_dec, entry, precision=precise)
    target = beta_rows[:, :, None] * (value_rows - predicted)
    update = low_product('hij,hjv->hiv', wy_rows, target)
    scores = low_product('hid,hjd->hij', query_dec, key_inv) * lower
    output = jnp.einsum('hld,hdv->hlv', query_dec, entry, precision=precise)
    output = output + low_product('hij,hjv->hiv', scores, update)
    carried = jnp.exp(final[:, 0, :])[:, :, None] * entry
    carried = carried + low_product('hld,hlv->hdv', key_tail, update)
    return (carried, output)

def core(query_unit, key_unit, value_f, decay, beta, wy_inverse, keep, state, stepper):
    heads = beta.shape[0]
    count = query_unit.shape[0] // GROUP
    blocks = (to_blocks(query_unit, heads, DK), to_blocks(key_unit, heads, DK), to_blocks(value_f, heads, DV), to_blocks(decay, heads, DK), beta.reshape(heads, count, GROUP).transpose(1, 0, 2), wy_inverse.reshape(count, GROUP, heads, GROUP).transpose(0, 2, 1, 3), keep)
    final, outputs = lax.scan(stepper, state, blocks)
    return (from_blocks(outputs), final)

def gated_norm(output, gate, gain):
    rows = output.reshape(output.shape[0], -1, DV)
    scale = lax.rsqrt(lax.optimization_barrier(jnp.mean(rows * rows, axis=-1, keepdims=True)) + 1e-06)
    gates = jax.nn.sigmoid(gate.reshape(rows.shape))
    return (rows * scale * gain * gates).reshape(output.shape)

def reference(queries, keys, values, decay, beta, wy_inverse, out_gate, norm_gain, out_proj, grad_out, resets):
    upstream = jnp.dot(grad_out, out_proj.T, preferred_element_type=jnp.float32)
    count = queries.shape[0] // GROUP
    blocks_idx = jnp.arange(count)
    starts = resets[(blocks_idx // CH_DEV).astype(jnp.int32)]
    keep = ((blocks_idx % CH_DEV).astype(jnp.int32) != starts).astype(jnp.float32)
    anchor = jnp.zeros((H, DK, DV), jnp.float32)
    stepper = jax.checkpoint(group_step)

    def layer(query_f, key_f, value_f, gate_log, beta_f, gate_f):
        query_unit = unit_rows(query_f, DK, DK ** (-0.5))
        key_unit = unit_rows(key_f, DK, 1.0)
        output, final = core(query_unit, key_unit, value_f, gate_log, beta_f, wy_inverse, keep, anchor, stepper)
        return gated_norm(output, gate_f, norm_gain)
    normed, pullback = jax.vjp(layer, queries.astype(jnp.float32), keys.astype(jnp.float32), values.astype(jnp.float32), decay, beta, out_gate.astype(jnp.float32))
    grads = pullback(upstream)
    return (grads[0].astype(jnp.bfloat16), grads[1].astype(jnp.bfloat16), grads[2].astype(jnp.bfloat16), grads[3], grads[4], grads[5].astype(jnp.bfloat16))
```

```python
import functools

import jax
import jax.numpy as jnp
from jax import lax
from jax.experimental import pallas as pl
from jax.experimental.pallas import tpu as pltpu
from jax.sharding import PartitionSpec as P

DK = 128
DV = 128
GROUP = 64
EPS = 1e-6
SCALE = DK**-0.5
STEP = 2
RING = 4

f32 = jnp.float32
bf16 = jnp.bfloat16


def nn(a, b):
    return lax.dot_general(a, b, (((1,), (0,)), ((), ())), preferred_element_type=f32)


def nt(a, b):
    return lax.dot_general(a, b, (((1,), (1,)), ((), ())), preferred_element_type=f32)


def tn(a, b):
    return lax.dot_general(a, b, (((0,), (0,)), ((), ())), preferred_element_type=f32)


def triangle(upper, dtype):
    row = lax.broadcasted_iota(jnp.int32, (GROUP, GROUP), 0)
    col = lax.broadcasted_iota(jnp.int32, (GROUP, GROUP), 1)
    return (row <= col if upper else row >= col).astype(dtype)


def sum_rows(weights, x):
    high = x.astype(bf16)
    low = (x - high.astype(f32)).astype(bf16)
    return nn(weights, jnp.concatenate([high, low], axis=0))


def twice(upper):
    t = triangle(upper, f32)
    return jnp.concatenate([t, t], axis=1).astype(bf16)


def inverse_norm(x):
    return lax.rsqrt(jnp.sum(x * x, axis=-1, keepdims=True) + EPS)


def cols(h):
    return slice(128 * h, 128 * h + 128)


def half(h):
    return slice(64 * h, 64 * h + 64)


def kernel_a1(
    heads, resets, k_ref, v_ref, d_ref, b_ref, w_ref,
    g_ref, wb_ref, kd_ref, kt_ref, y_ref, n_ref, pre_ref, mb_ref, state,
):
    step = pl.program_id(0)

    @pl.when(step == 0)
    def _():
        row = lax.broadcasted_iota(jnp.int32, (256, 128), 0)
        col = lax.broadcasted_iota(jnp.int32, (256, 128), 1)
        for h in range(heads):
            state[h] = (row == col + 128).astype(f32)

    weights = twice(False)
    for c in range(STEP):
        rows = half(c)
        keep = (step * STEP + c != resets[0]).astype(f32)
        gamma = sum_rows(weights, d_ref[rows, :])
        g_ref[rows, :] = gamma
        for h in range(heads):
            g = gamma[:, cols(h)]
            last = g[63:64, :]
            k = k_ref[rows, cols(h)].astype(f32)
            ku = k * inverse_norm(k)
            kd = (ku * jnp.exp(g)).astype(bf16)
            kt = (ku * jnp.exp(last - g)).astype(bf16)
            wb = (w_ref[c, :, half(h)] * b_ref[h : h + 1, half(c)]).astype(bf16)
            xy = nn(wb, jnp.concatenate([v_ref[rows, cols(h)], kd], axis=1)).astype(bf16)
            bn = tn(xy, kt)
            n = bn[128:].astype(bf16)
            r = state[h] * keep
            rb = r.astype(bf16)
            r = jnp.exp(last) * r - nn(rb, n)
            state[h, 0:128] = r[0:128] + bn[0:128]
            state[h, 128:256] = r[128:256]
            wb_ref[c, :, half(h)] = wb
            kd_ref[rows, cols(h)] = kd
            kt_ref[rows, cols(h)] = kt
            y_ref[rows, cols(h)] = xy[:, 128:]
            n_ref[c, h] = n
            pre_ref[c, h] = rb

    @pl.when(step == pl.num_programs(0) - 1)
    def _():
        mb_ref[...] = state[...].astype(bf16)


def kernel_a2(heads, q_ref, k_ref, g_ref, qd_ref, ki_ref, a_ref, at_ref):
    lower = triangle(False, f32)
    upper = triangle(True, f32)
    for c in range(STEP):
        rows = half(c)
        for h in range(heads):
            g = g_ref[rows, cols(h)]
            q = q_ref[rows, cols(h)].astype(f32)
            k = k_ref[rows, cols(h)].astype(f32)
            qd = (q * (inverse_norm(q) * SCALE) * jnp.exp(g)).astype(bf16)
            ki = (k * inverse_norm(k) * jnp.exp(-g)).astype(bf16)
            qd_ref[rows, cols(h)] = qd
            ki_ref[rows, cols(h)] = ki
            a_ref[c, :, half(h)] = (nt(qd, ki) * lower).astype(bf16)
            at_ref[c, :, half(h)] = (nt(ki, qd) * upper).astype(bf16)


def kernel_b(
    heads, v_ref, kd_ref, qd_ref, y_ref, wb_ref, a_ref, at_ref, pre_ref, gate_ref, up_ref, gain_ref, s_ref,
    e_ref, vp_ref, u_ref, do_ref, du_ref, dt_ref, dg_ref, r_ref, total,
):
    step = pl.program_id(0)

    @pl.when(step == 0)
    def _():
        total[...] = jnp.zeros_like(total)

    gain = gain_ref[...]
    for c in range(STEP):
        rows = half(c)
        for h in range(heads):
            m = pre_ref[c, h, 128:256]
            e = (pre_ref[c, h, 0:128].astype(f32) + nn(s_ref[h], m)).astype(bf16)
            e_ref[c, h] = e
            qd = qd_ref[rows, cols(h)]
            both = nt(jnp.concatenate([kd_ref[rows, cols(h)], qd], axis=0), e)
            vp = (v_ref[rows, cols(h)].astype(f32) - both[0:64]).astype(bf16)
            u = nn(wb_ref[c, :, half(h)], vp).astype(bf16)
            o = both[64:128] + nn(a_ref[c, :, half(h)], u)
            rms = lax.rsqrt(jnp.mean(o * o, axis=-1, keepdims=True) + EPS)
            sig = jax.nn.sigmoid(gate_ref[rows, cols(h)].astype(f32))
            w = up_ref[rows, cols(h)].astype(f32) * gain * sig
            on = o * rms
            won = w * on
            dg_ref[rows, cols(h)] = (won * (1.0 - sig)).astype(bf16)
            do = (rms * (w - on * jnp.mean(won, axis=-1, keepdims=True))).astype(bf16)
            du = nn(at_ref[c, :, half(h)], do).astype(bf16)
            dt = tn(
                jnp.concatenate([do, du], axis=0),
                jnp.concatenate([qd, -y_ref[rows, cols(h)]], axis=0),
            ).astype(bf16)
            total[h] += nt(dt, m)
            vp_ref[rows, cols(h)] = vp
            u_ref[rows, cols(h)] = u
            do_ref[rows, cols(h)] = do
            du_ref[rows, cols(h)] = du
            dt_ref[c, h] = dt

    @pl.when(step == pl.num_programs(0) - 1)
    def _():
        r_ref[...] = total[...].astype(bf16)


def kernel_c1(heads, q_ref, k_ref, g_ref, qd_ref, ki_ref, u_ref, do_ref, e_ref, dq_ref, dgam_ref, kk_ref):
    lower = triangle(False, f32)
    upper = triangle(True, f32)
    for c in range(STEP):
        rows = half(c)
        for h in range(heads):
            u = u_ref[rows, cols(h)]
            do = do_ref[rows, cols(h)]
            da = (nt(do, u) * lower).astype(bf16)
            dat = (nt(u, do) * upper).astype(bf16)
            g = g_ref[rows, cols(h)]
            dqu = (nn(do, e_ref[c, h]) + nn(da, ki_ref[rows, cols(h)])) * jnp.exp(g)
            dku = nn(dat, qd_ref[rows, cols(h)]) * jnp.exp(-g)
            q = q_ref[rows, cols(h)].astype(f32)
            k = k_ref[rows, cols(h)].astype(f32)
            rq = inverse_norm(q)
            qn = q * rq
            prod = qn * dqu
            along = jnp.sum(prod, axis=-1, keepdims=True)
            dq_ref[rows, cols(h)] = ((rq * SCALE) * (dqu - qn * along)).astype(bf16)
            dgam_ref[rows, cols(h)] = prod * SCALE - (k * inverse_norm(k)) * dku
            kk_ref[rows, cols(h)] = dku.astype(bf16)


def kernel_c2(
    heads, resets, k_ref, g_ref, b_ref, wb_ref, kt_ref, n_ref, e_ref, vp_ref, u_ref, du_ref, dt_ref,
    dgam_ref, kk_ref, gin_ref, dk_ref, dv_ref, dd_ref, db_ref, state,
):
    step = pl.program_id(0)
    place = pl.num_programs(0) - 1 - step

    @pl.when(step == 0)
    def _():
        state[...] = gin_ref[...].astype(f32)

    weights = twice(True)
    ones = jnp.ones((16, 128), bf16)
    for c in reversed(range(STEP)):
        rows = half(c)
        keep = (place * STEP + c != resets[0]).astype(f32)
        for h in range(heads):
            grad = state[h]
            gb = grad.astype(bf16)
            e = e_ref[c, h]
            u = u_ref[rows, cols(h)]
            g = g_ref[rows, cols(h)]
            last = g[63:64, :]
            lam = jnp.exp(last)
            state[h] = keep * (dt_ref[c, h].astype(f32) + lam * grad - nt(gb, n_ref[c, h]))
            du = (du_ref[rows, cols(h)].astype(f32) + nt(kt_ref[rows, cols(h)], gb)).astype(bf16)
            dv = tn(wb_ref[c, :, half(h)], du)
            dvb = dv.astype(bf16)
            dv_ref[rows, cols(h)] = dvb
            weighed = (dv * vp_ref[rows, cols(h)].astype(f32)).astype(bf16)
            db_ref[h : h + 1, half(c)] = nt(ones, weighed)[0:1] / b_ref[h : h + 1, half(c)]
            kdd = nn(dvb, e) * jnp.exp(g)
            ktt = nn(u, gb) * jnp.exp(last - g)
            k = k_ref[rows, cols(h)].astype(f32)
            rk = inverse_norm(k)
            ku = k * rk
            dku = kk_ref[rows, cols(h)].astype(f32) + ktt - kdd
            along = jnp.sum(ku * dku, axis=-1, keepdims=True)
            dk_ref[rows, cols(h)] = (rk * (dku - ku * along)).astype(bf16)
            kutt = ku * ktt
            dgam = dgam_ref[rows, cols(h)] - ku * kdd - kutt
            dlast = jnp.sum(kutt, axis=0, keepdims=True) + lam * jnp.sum(
                grad * e.astype(f32), axis=0, keepdims=True
            )
            dd_ref[rows, cols(h)] = sum_rows(weights, dgam) + dlast


def gather_slots(me, own, others, slots, part=slice(None)):
    slots[me] = own[:, part]
    for shift, other in enumerate(others, 1):
        slots[lax.rem(me + RING - shift, RING)] = other[:, part]


def kernel_f1(heads, place, own, p1, p2, p3, total_ref, slots):
    gather_slots(place[1], own, (p1, p2, p3), slots)
    for h in range(heads):
        r = slots[0, h].astype(f32)
        for z in range(1, RING):
            r = nn(r.astype(bf16), slots[z, h, 128:256])
            r = jnp.concatenate([r[0:128] + slots[z, h, 0:128].astype(f32), r[128:256]], axis=0)
        total_ref[h] = r.astype(bf16)
    return


def kernel_f2(heads, place, own, p1, p2, p3, zslots, s_ref, yslots):
    gather_slots(place[0], own, (p1, p2, p3), yslots)
    for h in range(heads):
        s = jnp.zeros((DV, DK), f32)
        for slots, me in ((yslots, place[0]), (zslots, place[1])):
            for i in range(RING - 1):
                moved = nn(s.astype(bf16), slots[i, h, 128:256]) + slots[i, h, 0:128].astype(f32)
                s = jnp.where(i < me, moved, s)
        s_ref[h] = s.astype(bf16)


def kernel_r1(heads, place, own, p1, p2, p3, zslots, total_ref, slots):
    gather_slots(place[1], own, (p1, p2, p3), slots)
    for h in range(heads):
        g = slots[RING - 1, h].astype(f32)
        for z in reversed(range(RING - 1)):
            g = nt(g.astype(bf16), zslots[z, h, 128:256]) + slots[z, h].astype(f32)
        total_ref[h] = g.astype(bf16)


def kernel_r2(heads, place, own, p1, p2, p3, zr, zslots, yslots, g_ref, yr):
    gather_slots(place[0], own, (p1, p2, p3), yr)
    for h in range(heads):
        g = jnp.zeros((DV, DK), f32)
        for grads, slots, me in ((yr, yslots, place[0]), (zr, zslots, place[1])):
            for i in reversed(range(1, RING)):
                moved = nt(g.astype(bf16), slots[i, h, 128:256]) + grads[i, h].astype(f32)
                g = jnp.where(i > me, moved, g)
        g_ref[h] = g.astype(bf16)


def permute(x, distance, outer):
    size = lax.axis_size("seq")
    if outer:
        pairs = [(i, (i + RING * distance) % size) for i in range(size)]
    else:
        pairs = [(i, i // RING * RING + (i + distance) % RING) for i in range(size)]
    return lax.ppermute(x, "seq", pairs)


def three(x, outer):
    return [permute(x, distance, outer) for distance in (1, 2, 3)]


SMEM = pl.BlockSpec(memory_space=pltpu.SMEM)
VMEM = pl.BlockSpec(memory_space=pltpu.VMEM)


def shape(dims, dtype):
    return jax.ShapeDtypeStruct(dims, dtype)


def call(body, name, heads, in_specs, out_specs, out_shape, scratch, grid, flops, *args):
    total = sum(a.size * a.dtype.itemsize for a in args)
    total += sum(o.size * o.dtype.itemsize for o in out_shape)
    return pl.pallas_call(
        functools.partial(body, heads),
        out_shape=out_shape,
        grid=grid,
        in_specs=in_specs,
        out_specs=out_specs,
        scratch_shapes=scratch,
        compiler_params=pltpu.CompilerParams(
            vmem_limit_bytes=40 * 2**20,
            **({"dimension_semantics": ("arbitrary",)} if grid else {}),
        ),
        cost_estimate=pl.CostEstimate(flops=flops, bytes_accessed=total, transcendentals=0),
        name=name,
    )(*args)


def per_device(
    queries, keys, values, decay, beta, wy_inverse, out_gate, norm_gain, out_proj, grad_out, resets
):
    tokens = queries.shape[0]
    heads = beta.shape[0]
    count = tokens // GROUP
    steps = count // STEP
    width = heads * 128
    index = lax.axis_index("seq")
    place = jnp.stack([index // RING, index % RING]).astype(jnp.int32)
    upstream = lax.dot_general(
        lax.all_gather(grad_out, "head", axis=1, tiled=True),
        out_proj,
        (((1,), (1,)), ((), ())),
        preferred_element_type=f32,
    ).astype(bf16)

    def specs(back):
        at = (lambda i: steps - 1 - i) if back else (lambda i: i)
        return dict(
            tok=pl.BlockSpec((STEP * GROUP, width), lambda i: (at(i), 0)),
            beta=pl.BlockSpec((heads, STEP * GROUP), lambda i: (0, at(i))),
            wy=pl.BlockSpec((STEP, GROUP, heads * GROUP), lambda i: (at(i), 0, 0)),
            state=pl.BlockSpec((STEP, heads, 128, 128), lambda i: (at(i), 0, 0, 0)),
            pair=pl.BlockSpec((STEP, heads, 256, 128), lambda i: (at(i), 0, 0, 0)),
            whole=pl.BlockSpec((heads, 128, 128), lambda i: (0, 0, 0)),
            whole2=pl.BlockSpec((heads, 256, 128), lambda i: (0, 0, 0)),
            gain=pl.BlockSpec((1, 128), lambda i: (0, 0)),
        )

    s = specs(False)
    tok_b = shape((tokens, width), bf16)
    tok_f = shape((tokens, width), f32)
    small_b = shape((count, GROUP, heads * GROUP), bf16)
    state_b = shape((count, heads, 128, 128), bf16)
    pair_b = shape((count, heads, 256, 128), bf16)
    one_b = shape((heads, 128, 128), bf16)
    two_b = shape((heads, 256, 128), bf16)
    unit = count * heads * 2 * 64 * 128 * 128

    gamma, wb, kd, kt, y, n, pre, mb = call(
        kernel_a1, "a1", heads,
        [SMEM, s["tok"], s["tok"], s["tok"], s["beta"], s["wy"]],
        [s["tok"], s["wy"], s["tok"], s["tok"], s["tok"], s["state"], s["pair"], s["whole2"]],
        [tok_f, small_b, tok_b, tok_b, tok_b, state_b, pair_b, two_b],
        [pltpu.VMEM((heads, 256, 128), f32)], (steps,), 8 * unit,
        resets, keys, values, decay, beta, wy_inverse,
    )
    zs = three(mb, False)
    qd, ki, a, at = call(
        kernel_a2, "a2", heads,
        [s["tok"], s["tok"], s["tok"]],
        [s["tok"], s["tok"], s["wy"], s["wy"]],
        [tok_b, tok_b, small_b, small_b],
        [], (steps,), 2 * unit, queries, keys, gamma,
    )
    slots_b = shape((RING, heads, 256, 128), bf16)
    group, zslots = call(
        kernel_f1, "f1", heads, [SMEM] + [VMEM] * 4, [VMEM, VMEM], [two_b, slots_b], [], (),
        unit // 4, place, mb, *zs,
    )
    ys = three(group, True)
    state_in, yslots = call(
        kernel_f2, "f2", heads, [SMEM] + [VMEM] * 5, [VMEM, VMEM], [one_b, slots_b], [], (),
        unit // 4, place, group, *ys, zslots,
    )
    e, vp, u, do, du, dt, dgate, r = call(
        kernel_b, "b", heads,
        [s["tok"], s["tok"], s["tok"], s["tok"], s["wy"], s["wy"], s["wy"], s["pair"], s["tok"], s["tok"], s["gain"], s["whole"]],
        [s["state"], s["tok"], s["tok"], s["tok"], s["tok"], s["state"], s["tok"], s["whole"]],
        [state_b, tok_b, tok_b, tok_b, tok_b, state_b, tok_b, one_b],
        [pltpu.VMEM((heads, 128, 128), f32)], (steps,), 12 * unit,
        values, kd, qd, y, wb, a, at, pre, out_gate, upstream, norm_gain.reshape(1, 128), state_in,
    )
    zr = three(r, False)
    dq, dgam, kk = call(
        kernel_c1, "c1", heads,
        [s["tok"]] * 7 + [s["state"]],
        [s["tok"], s["tok"], s["tok"]], [tok_b, tok_f, tok_b],
        [], (steps,), 4 * unit, queries, keys, gamma, qd, ki, u, do, e,
    )
    rslots_b = shape((RING, heads, 128, 128), bf16)
    rgroup, rslots = call(
        kernel_r1, "r1", heads, [SMEM] + [VMEM] * 5, [VMEM, VMEM], [one_b, rslots_b], [], (),
        unit // 4, place, r, *zr, zslots,
    )
    yr = three(rgroup, True)
    grad_in, _ = call(
        kernel_r2, "r2", heads, [SMEM] + [VMEM] * 7, [VMEM, VMEM], [one_b, rslots_b], [], (),
        unit // 4, place, rgroup, *yr, rslots, zslots, yslots,
    )
    t = specs(True)
    dk, dv, dd, db = call(
        kernel_c2, "c2", heads,
        [SMEM, t["tok"], t["tok"], t["beta"], t["wy"], t["tok"], t["state"], t["state"], t["tok"], t["tok"], t["tok"], t["state"], t["tok"], t["tok"], t["whole"]],
        [t["tok"], t["tok"], t["tok"], t["beta"]],
        [tok_b, tok_b, tok_f, shape((heads, tokens), f32)],
        [pltpu.VMEM((heads, 128, 128), f32)], (steps,), 10 * unit,
        resets, keys, gamma, beta, wb, kt, n, e, vp, u, du, dt, dgam, kk, grad_in,
    )
    return dq, dk, dv, dd, db, dgate


def solution(mesh):
    return jax.shard_map(
        per_device,
        mesh=mesh,
        in_specs=(
            P("seq", "head"),
            P("seq", "head"),
            P("seq", "head"),
            P("seq", "head"),
            P("head", "seq"),
            P("seq", None, "head"),
            P("seq", "head"),
            P(),
            P("head", None),
            P("seq", "head"),
            P("seq"),
        ),
        out_specs=(
            P("seq", "head"),
            P("seq", "head"),
            P("seq", "head"),
            P("seq", "head"),
            P("head", "seq"),
            P("seq", "head"),
        ),
        check_vma=False,
    )
```

```python
import functools

import jax
import jax.numpy as jnp
from jax import lax
from jax.experimental import pallas as pl
from jax.experimental.pallas import tpu as pltpu
from jax.sharding import PartitionSpec as P

DK = 128
DV = 128
GROUP = 64
EPS = 1e-6
SCALE = DK**-0.5
STEP = 4
UNITS = dict(a1=16, a2=16, b=16, c0=16, c1=16, c2=16)
RING = 4

f32 = jnp.float32
bf16 = jnp.bfloat16


def nn(a, b):
    return lax.dot_general(a, b, (((1,), (0,)), ((), ())), preferred_element_type=f32)


def nt(a, b):
    return lax.dot_general(a, b, (((1,), (1,)), ((), ())), preferred_element_type=f32)


def tn(a, b):
    return lax.dot_general(a, b, (((0,), (0,)), ((), ())), preferred_element_type=f32)


def triangle(upper, dtype):
    row = lax.broadcasted_iota(jnp.int32, (GROUP, GROUP), 0)
    col = lax.broadcasted_iota(jnp.int32, (GROUP, GROUP), 1)
    return (row <= col if upper else row >= col).astype(dtype)


def sum_rows(weights, x):
    high = x.astype(bf16)
    low = (x - high.astype(f32)).astype(bf16)
    return nn(weights, jnp.concatenate([high, low], axis=0))


def twice(upper):
    t = triangle(upper, f32)
    return jnp.concatenate([t, t], axis=1).astype(bf16)


def inverse_norm(x):
    return lax.rsqrt(jnp.sum(x * x, axis=-1, keepdims=True) + EPS)


def cols(h):
    return slice(128 * h, 128 * h + 128)


def half(h):
    return slice(64 * h, 64 * h + 64)


def units(heads, size):
    pairs = [(c, h) for c in range(STEP) for h in range(heads)]
    return [pairs[i : i + size] for i in range(0, len(pairs), size)]


def each(f, *lists):
    return [f(*xs) for xs in zip(*lists)]


def kernel_a1(
    heads, resets, k_ref, v_ref, d_ref, b_ref, w_ref,
    g_ref, wb_ref, kd_ref, kt_ref, y_ref, n_ref, pre_ref, mb_ref, state,
):
    step = pl.program_id(0)

    @pl.when(step == 0)
    def _():
        row = lax.broadcasted_iota(jnp.int32, (256, 128), 0)
        col = lax.broadcasted_iota(jnp.int32, (256, 128), 1)
        for h in range(heads):
            state[h] = (row == col + 128).astype(f32)

    weights = twice(False)
    gammas = [sum_rows(weights, d_ref[half(c), :]) for c in range(STEP)]
    for c in range(STEP):
        g_ref[half(c), :] = gammas[c]
    rs = [state[h] for h in range(heads)]
    for group in units(heads, UNITS["a1"]):
        gs = [gammas[c][:, cols(h)] for c, h in group]
        ks = [k_ref[half(c), cols(h)].astype(f32) for c, h in group]
        kus = each(lambda k: k * inverse_norm(k), ks)
        kds = each(lambda ku, g: (ku * jnp.exp(g)).astype(bf16), kus, gs)
        kts = each(lambda ku, g: (ku * jnp.exp(g[63:64, :] - g)).astype(bf16), kus, gs)
        wbs = [(w_ref[c, :, half(h)] * b_ref[h : h + 1, half(c)]).astype(bf16) for c, h in group]
        xys = [
            nn(wb, jnp.concatenate([v_ref[half(c), cols(h)], kd], axis=1)).astype(bf16)
            for wb, kd, (c, h) in zip(wbs, kds, group)
        ]
        bns = each(tn, xys, kts)
        ns = each(lambda bn: bn[128:].astype(bf16), bns)
        for (c, h), wb, kd, kt, xy, n in zip(group, wbs, kds, kts, xys, ns):
            wb_ref[c, :, half(h)] = wb
            kd_ref[half(c), cols(h)] = kd
            kt_ref[half(c), cols(h)] = kt
            y_ref[half(c), cols(h)] = xy[:, 128:]
            n_ref[c, h] = n
        for (c, h), bn, n, g in zip(group, bns, ns, gs):
            keep = (step * STEP + c != resets[0]).astype(f32)
            r = rs[h] * keep
            rb = r.astype(bf16)
            pre_ref[c, h] = rb
            r = jnp.exp(g[63:64, :]) * r - nn(rb, n)
            rs[h] = jnp.concatenate([r[0:128] + bn[0:128], r[128:256]], axis=0)
    for h in range(heads):
        state[h] = rs[h]

    @pl.when(step == pl.num_programs(0) - 1)
    def _():
        for h in range(heads):
            mb_ref[h] = rs[h].astype(bf16)


def kernel_a2(heads, q_ref, k_ref, g_ref, qd_ref, ki_ref, a_ref, at_ref):
    lower = triangle(False, f32)
    upper = triangle(True, f32)
    for group in units(heads, UNITS["a2"]):
        gs = [g_ref[half(c), cols(h)] for c, h in group]
        qs = [q_ref[half(c), cols(h)].astype(f32) for c, h in group]
        ks = [k_ref[half(c), cols(h)].astype(f32) for c, h in group]
        qds = each(lambda q, g: (q * (inverse_norm(q) * SCALE) * jnp.exp(g)).astype(bf16), qs, gs)
        kis = each(lambda k, g: (k * inverse_norm(k) * jnp.exp(-g)).astype(bf16), ks, gs)
        als = each(lambda qd, ki: (nt(qd, ki) * lower).astype(bf16), qds, kis)
        ats = each(lambda qd, ki: (nt(ki, qd) * upper).astype(bf16), qds, kis)
        for (c, h), qd, ki, a, at in zip(group, qds, kis, als, ats):
            qd_ref[half(c), cols(h)] = qd
            ki_ref[half(c), cols(h)] = ki
            a_ref[c, :, half(h)] = a
            at_ref[c, :, half(h)] = at


def kernel_b(
    heads, v_ref, kd_ref, qd_ref, y_ref, wb_ref, a_ref, at_ref, pre_ref, gate_ref, up_ref, gain_ref, s_ref,
    e_ref, vp_ref, u_ref, do_ref, du_ref, dt_ref, dg_ref, r_ref, total,
):
    step = pl.program_id(0)

    @pl.when(step == 0)
    def _():
        total[...] = jnp.zeros_like(total)

    gain = gain_ref[...]
    sums = [total[h] for h in range(heads)]
    for group in units(heads, UNITS["b"]):
        es = [
            (pre_ref[c, h, 0:128].astype(f32) + nn(s_ref[h], pre_ref[c, h, 128:256])).astype(bf16)
            for c, h in group
        ]
        boths = [
            nt(jnp.concatenate([kd_ref[half(c), cols(h)], qd_ref[half(c), cols(h)]], axis=0), e)
            for e, (c, h) in zip(es, group)
        ]
        vps = [
            (v_ref[half(c), cols(h)].astype(f32) - both[0:64]).astype(bf16)
            for both, (c, h) in zip(boths, group)
        ]
        us = [nn(wb_ref[c, :, half(h)], vp).astype(bf16) for vp, (c, h) in zip(vps, group)]
        os = [both[64:128] + nn(a_ref[c, :, half(h)], u) for both, u, (c, h) in zip(boths, us, group)]
        rmss = each(lambda o: lax.rsqrt(jnp.mean(o * o, axis=-1, keepdims=True) + EPS), os)
        sigs = [jax.nn.sigmoid(gate_ref[half(c), cols(h)].astype(f32)) for c, h in group]
        ws = [up_ref[half(c), cols(h)].astype(f32) * gain * sig for sig, (c, h) in zip(sigs, group)]
        ons = each(lambda o, rms: o * rms, os, rmss)
        wons = each(lambda w, on: w * on, ws, ons)
        dgs = each(lambda won, sig: (won * (1.0 - sig)).astype(bf16), wons, sigs)
        dos = each(
            lambda rms, w, on, won: (rms * (w - on * jnp.mean(won, axis=-1, keepdims=True))).astype(bf16),
            rmss, ws, ons, wons,
        )
        dus = [nn(at_ref[c, :, half(h)], do).astype(bf16) for do, (c, h) in zip(dos, group)]
        dts = [
            tn(
                jnp.concatenate([do, du], axis=0),
                jnp.concatenate([qd_ref[half(c), cols(h)], -y_ref[half(c), cols(h)]], axis=0),
            ).astype(bf16)
            for do, du, (c, h) in zip(dos, dus, group)
        ]
        for (c, h), dt in zip(group, dts):
            sums[h] = sums[h] + nt(dt, pre_ref[c, h, 128:256])
        for (c, h), e, vp, u, do, du, dt, dg in zip(group, es, vps, us, dos, dus, dts, dgs):
            e_ref[c, h] = e
            vp_ref[half(c), cols(h)] = vp
            u_ref[half(c), cols(h)] = u
            do_ref[half(c), cols(h)] = do
            du_ref[half(c), cols(h)] = du
            dt_ref[c, h] = dt
            dg_ref[half(c), cols(h)] = dg
    for h in range(heads):
        total[h] = sums[h]

    @pl.when(step == pl.num_programs(0) - 1)
    def _():
        for h in range(heads):
            r_ref[h] = sums[h].astype(bf16)


def kernel_c1(heads, q_ref, g_ref, ki_ref, u_ref, do_ref, e_ref, dq_ref, pq_ref):
    lower = triangle(False, f32)
    for group in units(heads, UNITS["c1"]):
        us = [u_ref[half(c), cols(h)] for c, h in group]
        dos = [do_ref[half(c), cols(h)] for c, h in group]
        das = each(lambda do, u: (nt(do, u) * lower).astype(bf16), dos, us)
        dqus = [
            (nn(do, e_ref[c, h]) + nn(da, ki_ref[half(c), cols(h)])) * jnp.exp(g_ref[half(c), cols(h)])
            for do, da, (c, h) in zip(dos, das, group)
        ]
        qs = [q_ref[half(c), cols(h)].astype(f32) for c, h in group]
        rqs = each(lambda q: inverse_norm(q), qs)
        qns = each(lambda q, rq: q * rq, qs, rqs)
        prods = each(lambda qn, dqu: qn * dqu, qns, dqus)
        dqs = each(
            lambda rq, dqu, qn, prod: (
                (rq * SCALE) * (dqu - qn * jnp.sum(prod, axis=-1, keepdims=True))
            ).astype(bf16),
            rqs, dqus, qns, prods,
        )
        for (c, h), dq, prod in zip(group, dqs, prods):
            dq_ref[half(c), cols(h)] = dq
            pq_ref[half(c), cols(h)] = prod * SCALE


def kernel_c0(heads, g_ref, qd_ref, u_ref, do_ref, kk_ref):
    upper = triangle(True, f32)
    for group in units(heads, UNITS["c0"]):
        us = [u_ref[half(c), cols(h)] for c, h in group]
        dos = [do_ref[half(c), cols(h)] for c, h in group]
        dats = each(lambda do, u: (nt(u, do) * upper).astype(bf16), dos, us)
        dkus = [
            nn(dat, qd_ref[half(c), cols(h)]) * jnp.exp(-g_ref[half(c), cols(h)])
            for dat, (c, h) in zip(dats, group)
        ]
        for (c, h), dku in zip(group, dkus):
            kk_ref[half(c), cols(h)] = dku.astype(bf16)


def kernel_c2(
    heads, resets, k_ref, g_ref, b_ref, wb_ref, kt_ref, n_ref, e_ref, vp_ref, u_ref, du_ref, dt_ref,
    pq_ref, kk_ref, gin_ref, dk_ref, dv_ref, dd_ref, db_ref, state,
):
    step = pl.program_id(0)
    place = pl.num_programs(0) - 1 - step

    @pl.when(step == 0)
    def _():
        state[...] = gin_ref[...].astype(f32)

    weights = twice(True)
    ones = jnp.ones((16, 128), bf16)
    grads = {}
    gbs = {}
    now = [state[h] for h in range(heads)]
    for c in reversed(range(STEP)):
        keep = (place * STEP + c != resets[0]).astype(f32)
        for h in range(heads):
            grads[c, h] = now[h]
            gbs[c, h] = now[h].astype(bf16)
        for h in range(heads):
            lam = jnp.exp(g_ref[64 * c + 63 : 64 * c + 64, cols(h)])
            now[h] = keep * (dt_ref[c, h].astype(f32) + lam * now[h] - nt(gbs[c, h], n_ref[c, h]))
    for h in range(heads):
        state[h] = now[h]
    for group in reversed(units(heads, UNITS["c2"])):
        gb = [gbs[p] for p in group]
        dus = [
            (du_ref[half(c), cols(h)].astype(f32) + nt(kt_ref[half(c), cols(h)], x)).astype(bf16)
            for x, (c, h) in zip(gb, group)
        ]
        dvs = [tn(wb_ref[c, :, half(h)], du) for du, (c, h) in zip(dus, group)]
        dvbs = each(lambda x: x.astype(bf16), dvs)
        gs = [g_ref[half(c), cols(h)] for c, h in group]
        ktts = [
            nn(u_ref[half(c), cols(h)], x) * jnp.exp(g[63:64, :] - g) for x, g, (c, h) in zip(gb, gs, group)
        ]
        kdds = [nn(dvb, e_ref[c, h]) * jnp.exp(g) for dvb, g, (c, h) in zip(dvbs, gs, group)]
        ks = [k_ref[half(c), cols(h)].astype(f32) for c, h in group]
        rks = each(inverse_norm, ks)
        kus = each(lambda k, rk: k * rk, ks, rks)
        sums = [kk_ref[half(c), cols(h)].astype(f32) + ktt for ktt, (c, h) in zip(ktts, group)]
        dkus = each(lambda x, kdd: x - kdd, sums, kdds)
        dks = each(
            lambda rk, dku, ku: (rk * (dku - ku * jnp.sum(ku * dku, axis=-1, keepdims=True))).astype(bf16),
            rks, dkus, kus,
        )
        kutts = each(lambda ku, ktt: ku * ktt, kus, ktts)
        dgams = [
            pq_ref[half(c), cols(h)] - ku * (x + kdd) for ku, kdd, x, (c, h) in zip(kus, kdds, sums, group)
        ]
        dlasts = [
            jnp.sum(kutt, axis=0, keepdims=True)
            + jnp.exp(g[63:64, :]) * jnp.sum(grads[c, h] * e_ref[c, h].astype(f32), axis=0, keepdims=True)
            for kutt, g, (c, h) in zip(kutts, gs, group)
        ]
        dds = each(lambda dgam, dlast: sum_rows(weights, dgam) + dlast, dgams, dlasts)
        dbs = [
            nt(ones, (dv * vp_ref[half(c), cols(h)].astype(f32)).astype(bf16))[0:1]
            for dv, (c, h) in zip(dvs, group)
        ]
        for (c, h), dvb, dk, dd, db in zip(group, dvbs, dks, dds, dbs):
            dv_ref[half(c), cols(h)] = dvb
            dk_ref[half(c), cols(h)] = dk
            dd_ref[half(c), cols(h)] = dd
            db_ref[h : h + 1, half(c)] = db / b_ref[h : h + 1, half(c)]


def gather_slots(me, own, others, slots):
    slots[me] = own[...]
    for shift, other in enumerate(others, 1):
        slots[lax.rem(me + RING - shift, RING)] = other[...]


def identity_pair():
    row = lax.broadcasted_iota(jnp.int32, (256, 128), 0)
    col = lax.broadcasted_iota(jnp.int32, (256, 128), 1)
    return (row == col + 128).astype(f32)


def after(pair, r):
    moved = nn(r.astype(bf16), pair[128:256])
    return jnp.concatenate([moved[0:128] + pair[0:128].astype(f32), moved[128:256]], axis=0)


def kernel_f1(heads, place, own, p1, p2, p3, total_ref, before_ref, slots):
    me = place[1]
    gather_slots(me, own, (p1, p2, p3), slots)
    start = identity_pair()
    rs = [slots[0, h].astype(f32) for h in range(heads)]
    befores = [jnp.where(me == 0, start, r) for r in rs]
    for z in range(1, RING):
        befores = [jnp.where(z < me, after(slots[z, h], r), b) for h, (r, b) in enumerate(zip(rs, befores))]
        rs = [after(slots[z, h], r) for h, r in enumerate(rs)]
    for h in range(heads):
        total_ref[h] = rs[h].astype(bf16)
        before_ref[h] = befores[h].astype(bf16)


def kernel_f2(heads, place, own, p1, p2, p3, before, s_ref, slots):
    me = place[0]
    gather_slots(me, own, (p1, p2, p3), slots)
    ss = [jnp.where(me > 0, slots[0, h, 0:128].astype(f32), 0.0) for h in range(heads)]
    for i in range(1, RING - 1):
        moved = [
            nn(s.astype(bf16), slots[i, h, 128:256]) + slots[i, h, 0:128].astype(f32) for h, s in enumerate(ss)
        ]
        ss = [jnp.where(i < me, m, s) for m, s in zip(moved, ss)]
    ss = [nn(s.astype(bf16), before[h, 128:256]) + before[h, 0:128].astype(f32) for h, s in enumerate(ss)]
    for h in range(heads):
        s_ref[h] = ss[h].astype(bf16)


def kernel_m(heads, place, zslots, m_ref):
    me = place[1]
    row = lax.broadcasted_iota(jnp.int32, (128, 128), 0)
    col = lax.broadcasted_iota(jnp.int32, (128, 128), 1)
    ms = [jnp.where(me < RING - 1, zslots[RING - 1, h, 128:256].astype(f32), (row == col).astype(f32)) for h in range(heads)]
    for i in reversed(range(1, RING - 1)):
        moved = [nn(zslots[i, h, 128:256], m.astype(bf16)) for h, m in enumerate(ms)]
        ms = [jnp.where(i > me, x, m) for x, m in zip(moved, ms)]
    for h in range(heads):
        m_ref[h] = ms[h].astype(bf16)


def kernel_r1(heads, place, own, p1, p2, p3, zslots, total_ref, later_ref, slots):
    me = place[1]
    gather_slots(me, own, (p1, p2, p3), slots)
    gs = [slots[RING - 1, h].astype(f32) for h in range(heads)]
    laters = [jnp.where(me < RING - 1, g, 0.0) for g in gs]
    for z in reversed(range(RING - 1)):
        gs = [nt(g.astype(bf16), zslots[z, h, 128:256]) + slots[z, h].astype(f32) for h, g in enumerate(gs)]
        laters = [jnp.where(z > me, g, x) for g, x in zip(gs, laters)]
    for h in range(heads):
        total_ref[h] = gs[h].astype(bf16)
        later_ref[h] = laters[h].astype(bf16)


def kernel_r2(heads, place, own, p1, p2, p3, later, later_m, yslots, g_ref, slots):
    me = place[0]
    gather_slots(me, own, (p1, p2, p3), slots)
    gs = [jnp.where(me < RING - 1, slots[RING - 1, h].astype(f32), 0.0) for h in range(heads)]
    for i in reversed(range(1, RING - 1)):
        moved = [nt(g.astype(bf16), yslots[i, h, 128:256]) + slots[i, h].astype(f32) for h, g in enumerate(gs)]
        gs = [jnp.where(i > me, m, g) for m, g in zip(moved, gs)]
    for h in range(heads):
        g_ref[h] = (nt(gs[h].astype(bf16), later_m[h]) + later[h].astype(f32)).astype(bf16)


def permute(x, distance, outer):
    size = lax.axis_size("seq")
    if outer:
        pairs = [(i, (i + RING * distance) % size) for i in range(size)]
    else:
        pairs = [(i, i // RING * RING + (i + distance) % RING) for i in range(size)]
    return lax.ppermute(x, "seq", pairs)


def three(x, outer):
    return [permute(x, distance, outer) for distance in (1, 2, 3)]


VMEM_LIMIT = 60 * 2**20
SMEM = pl.BlockSpec(memory_space=pltpu.SMEM)
VMEM = pl.BlockSpec(memory_space=pltpu.VMEM)


def shape(dims, dtype):
    return jax.ShapeDtypeStruct(dims, dtype)


def call(body, name, heads, in_specs, out_specs, out_shape, scratch, grid, flops, *args):
    total = sum(a.size * a.dtype.itemsize for a in args)
    total += sum(o.size * o.dtype.itemsize for o in out_shape)
    return pl.pallas_call(
        functools.partial(body, heads),
        out_shape=out_shape,
        grid=grid,
        in_specs=in_specs,
        out_specs=out_specs,
        scratch_shapes=scratch,
        compiler_params=pltpu.CompilerParams(
            vmem_limit_bytes=VMEM_LIMIT,
            **({"dimension_semantics": ("arbitrary",)} if grid else {}),
        ),
        cost_estimate=pl.CostEstimate(flops=flops, bytes_accessed=total, transcendentals=0),
        name=name,
    )(*args)


def per_device(
    queries, keys, values, decay, beta, wy_inverse, out_gate, norm_gain, out_proj, grad_out, resets
):
    tokens = queries.shape[0]
    heads = beta.shape[0]
    count = tokens // GROUP
    steps = count // STEP
    width = heads * 128
    index = lax.axis_index("seq")
    place = jnp.stack([index // RING, index % RING]).astype(jnp.int32)
    gathered = lax.all_gather(grad_out, "head", axis=1, tiled=True)

    def specs(back):
        at = (lambda i: steps - 1 - i) if back else (lambda i: i)
        return dict(
            tok=pl.BlockSpec((STEP * GROUP, width), lambda i: (at(i), 0)),
            beta=pl.BlockSpec((heads, STEP * GROUP), lambda i: (0, at(i))),
            wy=pl.BlockSpec((STEP, GROUP, heads * GROUP), lambda i: (at(i), 0, 0)),
            state=pl.BlockSpec((STEP, heads, 128, 128), lambda i: (at(i), 0, 0, 0)),
            pair=pl.BlockSpec((STEP, heads, 256, 128), lambda i: (at(i), 0, 0, 0)),
            whole=pl.BlockSpec((heads, 128, 128), lambda i: (0, 0, 0)),
            whole2=pl.BlockSpec((heads, 256, 128), lambda i: (0, 0, 0)),
            gain=pl.BlockSpec((1, 128), lambda i: (0, 0)),
        )

    s = specs(False)
    tok_b = shape((tokens, width), bf16)
    tok_f = shape((tokens, width), f32)
    small_b = shape((count, GROUP, heads * GROUP), bf16)
    state_b = shape((count, heads, 128, 128), bf16)
    pair_b = shape((count, heads, 256, 128), bf16)
    one_b = shape((heads, 128, 128), bf16)
    two_b = shape((heads, 256, 128), bf16)
    unit = count * heads * 2 * 64 * 128 * 128

    gamma, wb, kd, kt, y, n, pre, mb = call(
        kernel_a1, "a1", heads,
        [SMEM, s["tok"], s["tok"], s["tok"], s["beta"], s["wy"]],
        [s["tok"], s["wy"], s["tok"], s["tok"], s["tok"], s["state"], s["pair"], s["whole2"]],
        [tok_f, small_b, tok_b, tok_b, tok_b, state_b, pair_b, two_b],
        [pltpu.VMEM((heads, 256, 128), f32)], (steps,), 8 * unit,
        resets, keys, values, decay, beta, wy_inverse,
    )
    zs = three(mb, False)
    qd, ki, a, at = call(
        kernel_a2, "a2", heads,
        [s["tok"], s["tok"], s["tok"]],
        [s["tok"], s["tok"], s["wy"], s["wy"]],
        [tok_b, tok_b, small_b, small_b],
        [], (steps,), 2 * unit, queries, keys, gamma,
    )
    zs, qd = lax.optimization_barrier((zs, qd))
    slots_b = shape((RING, heads, 256, 128), bf16)
    group, before, zslots = call(
        kernel_f1, "f1", heads, [SMEM] + [VMEM] * 4, [VMEM] * 3, [two_b, two_b, slots_b], [], (),
        unit // 4, place, mb, *zs,
    )
    ys = three(group, True)
    (later_m,) = call(kernel_m, "m", heads, [SMEM, VMEM], [VMEM], [one_b], [], (), unit // 8, place, zslots)
    upstream = lax.dot_general(
        gathered, out_proj, (((1,), (1,)), ((), ())), preferred_element_type=f32
    ).astype(bf16)
    ys, upstream, later_m = lax.optimization_barrier((ys, upstream, later_m))
    state_in, yslots = call(
        kernel_f2, "f2", heads, [SMEM] + [VMEM] * 5, [VMEM] * 2, [one_b, slots_b], [], (),
        unit // 4, place, group, *ys, before,
    )
    e, vp, u, do, du, dt, dgate, r = call(
        kernel_b, "b", heads,
        [s["tok"], s["tok"], s["tok"], s["tok"], s["wy"], s["wy"], s["wy"], s["pair"], s["tok"], s["tok"], s["gain"], s["whole"]],
        [s["state"], s["tok"], s["tok"], s["tok"], s["tok"], s["state"], s["tok"], s["whole"]],
        [state_b, tok_b, tok_b, tok_b, tok_b, state_b, tok_b, one_b],
        [pltpu.VMEM((heads, 128, 128), f32)], (steps,), 12 * unit,
        values, kd, qd, y, wb, a, at, pre, out_gate, upstream, norm_gain.reshape(1, 128), state_in,
    )
    zr = three(r, False)
    (kk,) = call(
        kernel_c0, "c0", heads, [s["tok"]] * 4, [s["tok"]], [tok_b], [], (steps,), 2 * unit, gamma, qd, u, do,
    )
    zr, kk = lax.optimization_barrier((zr, kk))
    rslots_b = shape((RING, heads, 128, 128), bf16)
    rgroup, later, _ = call(
        kernel_r1, "r1", heads, [SMEM] + [VMEM] * 5, [VMEM] * 3, [one_b, one_b, rslots_b], [], (),
        unit // 4, place, r, *zr, zslots,
    )
    yr = three(rgroup, True)
    dq, pq = call(
        kernel_c1, "c1", heads,
        [s["tok"]] * 5 + [s["state"]],
        [s["tok"], s["tok"]], [tok_b, tok_f],
        [], (steps,), 4 * unit, queries, gamma, ki, u, do, e,
    )
    yr, pq = lax.optimization_barrier((yr, pq))
    grad_in, _ = call(
        kernel_r2, "r2", heads, [SMEM] + [VMEM] * 7, [VMEM] * 2, [one_b, rslots_b], [], (),
        unit // 4, place, rgroup, *yr, later, later_m, yslots,
    )
    t = specs(True)
    dk, dv, dd, db = call(
        kernel_c2, "c2", heads,
        [SMEM, t["tok"], t["tok"], t["beta"], t["wy"], t["tok"], t["state"], t["state"], t["tok"], t["tok"], t["tok"], t["state"], t["tok"], t["tok"], t["whole"]],
        [t["tok"], t["tok"], t["tok"], t["beta"]],
        [tok_b, tok_b, tok_f, shape((heads, tokens), f32)],
        [pltpu.VMEM((heads, 128, 128), f32)], (steps,), 10 * unit,
        resets, keys, gamma, beta, wb, kt, n, e, vp, u, du, dt, pq, kk, grad_in,
    )
    return dq, dk, dv, dd, db, dgate


def solution(mesh):
    return jax.shard_map(
        per_device,
        mesh=mesh,
        in_specs=(
            P("seq", "head"),
            P("seq", "head"),
            P("seq", "head"),
            P("seq", "head"),
            P("head", "seq"),
            P("seq", None, "head"),
            P("seq", "head"),
            P(),
            P("head", None),
            P("seq", "head"),
            P("seq"),
        ),
        out_specs=(
            P("seq", "head"),
            P("seq", "head"),
            P("seq", "head"),
            P("seq", "head"),
            P("head", "seq"),
            P("seq", "head"),
        ),
        check_vma=False,
    )
```

```python
import functools

import jax
import jax.numpy as jnp
from jax import lax
from jax.experimental import pallas as pl
from jax.experimental.pallas import tpu as pltpu
from jax.sharding import PartitionSpec as P

DK = 128
DV = 128
GROUP = 64
EPS = 1e-6
SCALE = DK**-0.5
STEP = 4
UNITS = dict(a1=16, a2=16, b=16, c0=16, c1=16, c2=16)
RING = 4

f32 = jnp.float32
bf16 = jnp.bfloat16


def nn(a, b):
    return lax.dot_general(a, b, (((1,), (0,)), ((), ())), preferred_element_type=f32)


def nt(a, b):
    return lax.dot_general(a, b, (((1,), (1,)), ((), ())), preferred_element_type=f32)


def tn(a, b):
    return lax.dot_general(a, b, (((0,), (0,)), ((), ())), preferred_element_type=f32)


def triangle(upper, dtype):
    row = lax.broadcasted_iota(jnp.int32, (GROUP, GROUP), 0)
    col = lax.broadcasted_iota(jnp.int32, (GROUP, GROUP), 1)
    return (row <= col if upper else row >= col).astype(dtype)


def sum_rows(weights, x):
    high = x.astype(bf16)
    low = (x - high.astype(f32)).astype(bf16)
    return nn(weights, jnp.concatenate([high, low], axis=0))


def twice(upper):
    t = triangle(upper, f32)
    return jnp.concatenate([t, t], axis=1).astype(bf16)


def inverse_norm(x):
    return lax.rsqrt(jnp.sum(x * x, axis=-1, keepdims=True) + EPS)


def cols(h):
    return slice(128 * h, 128 * h + 128)


def half(h):
    return slice(64 * h, 64 * h + 64)


def units(heads, size):
    pairs = [(c, h) for c in range(STEP) for h in range(heads)]
    return [pairs[i : i + size] for i in range(0, len(pairs), size)]


def each(f, *lists):
    return [f(*xs) for xs in zip(*lists)]


def spread(me, array, outs):
    for shift, out in enumerate(outs):
        out[...] = array[lax.rem(me + shift, RING)].astype(out.dtype)


def collect(me, array, arrived):
    for shift, other in enumerate(arrived):
        array[lax.rem(me + RING - shift, RING)] = other[...].astype(array.dtype)


def kernel_a1(
    heads, place, resets, k_ref, v_ref, d_ref, b_ref, w_ref,
    g_ref, wb_ref, kd_ref, kt_ref, y_ref, n_ref, pre_ref, o0, o1, o2, o3, state,
):
    step = pl.program_id(0)

    @pl.when(step == 0)
    def _():
        row = lax.broadcasted_iota(jnp.int32, (256, 128), 0)
        col = lax.broadcasted_iota(jnp.int32, (256, 128), 1)
        for h in range(heads):
            state[h] = (row == col + 128).astype(f32)

    weights = twice(False)
    gammas = [sum_rows(weights, d_ref[half(c), :]) for c in range(STEP)]
    for c in range(STEP):
        g_ref[half(c), :] = gammas[c]
    rs = [state[h] for h in range(heads)]
    for group in units(heads, UNITS["a1"]):
        gs = [gammas[c][:, cols(h)] for c, h in group]
        ks = [k_ref[half(c), cols(h)].astype(f32) for c, h in group]
        kus = each(lambda k: k * inverse_norm(k), ks)
        kds = each(lambda ku, g: (ku * jnp.exp(g)).astype(bf16), kus, gs)
        kts = each(lambda ku, g: (ku * jnp.exp(g[63:64, :] - g)).astype(bf16), kus, gs)
        wbs = [(w_ref[c, :, half(h)] * b_ref[h : h + 1, half(c)]).astype(bf16) for c, h in group]
        xys = [
            nn(wb, jnp.concatenate([v_ref[half(c), cols(h)], kd], axis=1)).astype(bf16)
            for wb, kd, (c, h) in zip(wbs, kds, group)
        ]
        bns = each(tn, xys, kts)
        ns = each(lambda bn: bn[128:].astype(bf16), bns)
        for (c, h), wb, kd, kt, xy, n in zip(group, wbs, kds, kts, xys, ns):
            wb_ref[c, :, half(h)] = wb
            kd_ref[half(c), cols(h)] = kd
            kt_ref[half(c), cols(h)] = kt
            y_ref[half(c), cols(h)] = xy[:, 128:]
            n_ref[c, h] = n
        for (c, h), bn, n, g in zip(group, bns, ns, gs):
            keep = (step * STEP + c != resets[0]).astype(f32)
            r = rs[h] * keep
            rb = r.astype(bf16)
            pre_ref[c, h] = rb
            r = jnp.exp(g[63:64, :]) * r - nn(rb, n)
            rs[h] = jnp.concatenate([r[0:128] + bn[0:128], r[128:256]], axis=0)
    for h in range(heads):
        state[h] = rs[h]

    @pl.when(step == pl.num_programs(0) - 1)
    def _():
        spread(place[1], state, (o0, o1, o2, o3))


def kernel_a2(heads, q_ref, k_ref, g_ref, qd_ref, ki_ref, a_ref, at_ref):
    lower = triangle(False, f32)
    upper = triangle(True, f32)
    for group in units(heads, UNITS["a2"]):
        gs = [g_ref[half(c), cols(h)] for c, h in group]
        qs = [q_ref[half(c), cols(h)].astype(f32) for c, h in group]
        ks = [k_ref[half(c), cols(h)].astype(f32) for c, h in group]
        qds = each(lambda q, g: (q * (inverse_norm(q) * SCALE) * jnp.exp(g)).astype(bf16), qs, gs)
        kis = each(lambda k, g: (k * inverse_norm(k) * jnp.exp(-g)).astype(bf16), ks, gs)
        als = each(lambda qd, ki: (nt(qd, ki) * lower).astype(bf16), qds, kis)
        ats = each(lambda qd, ki: (nt(ki, qd) * upper).astype(bf16), qds, kis)
        for (c, h), qd, ki, a, at in zip(group, qds, kis, als, ats):
            qd_ref[half(c), cols(h)] = qd
            ki_ref[half(c), cols(h)] = ki
            a_ref[c, :, half(h)] = a
            at_ref[c, :, half(h)] = at


def kernel_b(
    heads, place, v_ref, kd_ref, qd_ref, y_ref, wb_ref, a_ref, at_ref, pre_ref, gate_ref, up_ref, gain_ref,
    s0, s1, s2, s3, e_ref, vp_ref, u_ref, do_ref, du_ref, dt_ref, dg_ref, r0, r1, r2, r3, total, s_ref,
):
    step = pl.program_id(0)

    @pl.when(step == 0)
    def _():
        total[...] = jnp.zeros_like(total)
        collect(place[1], s_ref, (s0, s1, s2, s3))

    gain = gain_ref[...]
    sums = [total[h] for h in range(heads)]
    for group in units(heads, UNITS["b"]):
        es = [
            (pre_ref[c, h, 0:128].astype(f32) + nn(s_ref[h], pre_ref[c, h, 128:256])).astype(bf16)
            for c, h in group
        ]
        boths = [
            nt(jnp.concatenate([kd_ref[half(c), cols(h)], qd_ref[half(c), cols(h)]], axis=0), e)
            for e, (c, h) in zip(es, group)
        ]
        vps = [
            (v_ref[half(c), cols(h)].astype(f32) - both[0:64]).astype(bf16)
            for both, (c, h) in zip(boths, group)
        ]
        us = [nn(wb_ref[c, :, half(h)], vp).astype(bf16) for vp, (c, h) in zip(vps, group)]
        os = [both[64:128] + nn(a_ref[c, :, half(h)], u) for both, u, (c, h) in zip(boths, us, group)]
        rmss = each(lambda o: lax.rsqrt(jnp.mean(o * o, axis=-1, keepdims=True) + EPS), os)
        sigs = [jax.nn.sigmoid(gate_ref[half(c), cols(h)].astype(f32)) for c, h in group]
        ws = [up_ref[half(c), cols(h)].astype(f32) * gain * sig for sig, (c, h) in zip(sigs, group)]
        ons = each(lambda o, rms: o * rms, os, rmss)
        wons = each(lambda w, on: w * on, ws, ons)
        dgs = each(lambda won, sig: (won * (1.0 - sig)).astype(bf16), wons, sigs)
        dos = each(
            lambda rms, w, on, won: (rms * (w - on * jnp.mean(won, axis=-1, keepdims=True))).astype(bf16),
            rmss, ws, ons, wons,
        )
        dus = [nn(at_ref[c, :, half(h)], do).astype(bf16) for do, (c, h) in zip(dos, group)]
        dts = [
            tn(
                jnp.concatenate([do, du], axis=0),
                jnp.concatenate([qd_ref[half(c), cols(h)], -y_ref[half(c), cols(h)]], axis=0),
            ).astype(bf16)
            for do, du, (c, h) in zip(dos, dus, group)
        ]
        for (c, h), dt in zip(group, dts):
            sums[h] = sums[h] + nt(dt, pre_ref[c, h, 128:256])
        for (c, h), e, vp, u, do, du, dt, dg in zip(group, es, vps, us, dos, dus, dts, dgs):
            e_ref[c, h] = e
            vp_ref[half(c), cols(h)] = vp
            u_ref[half(c), cols(h)] = u
            do_ref[half(c), cols(h)] = do
            du_ref[half(c), cols(h)] = du
            dt_ref[c, h] = dt
            dg_ref[half(c), cols(h)] = dg
    for h in range(heads):
        total[h] = sums[h]

    @pl.when(step == pl.num_programs(0) - 1)
    def _():
        spread(place[1], total, (r0, r1, r2, r3))


def kernel_c1(heads, q_ref, g_ref, ki_ref, u_ref, do_ref, e_ref, dq_ref, pq_ref):
    lower = triangle(False, f32)
    for group in units(heads, UNITS["c1"]):
        us = [u_ref[half(c), cols(h)] for c, h in group]
        dos = [do_ref[half(c), cols(h)] for c, h in group]
        das = each(lambda do, u: (nt(do, u) * lower).astype(bf16), dos, us)
        dqus = [
            (nn(do, e_ref[c, h]) + nn(da, ki_ref[half(c), cols(h)])) * jnp.exp(g_ref[half(c), cols(h)])
            for do, da, (c, h) in zip(dos, das, group)
        ]
        qs = [q_ref[half(c), cols(h)].astype(f32) for c, h in group]
        rqs = each(lambda q: inverse_norm(q), qs)
        qns = each(lambda q, rq: q * rq, qs, rqs)
        prods = each(lambda qn, dqu: qn * dqu, qns, dqus)
        dqs = each(
            lambda rq, dqu, qn, prod: (
                (rq * SCALE) * (dqu - qn * jnp.sum(prod, axis=-1, keepdims=True))
            ).astype(bf16),
            rqs, dqus, qns, prods,
        )
        for (c, h), dq, prod in zip(group, dqs, prods):
            dq_ref[half(c), cols(h)] = dq
            pq_ref[half(c), cols(h)] = prod * SCALE


def kernel_c0(heads, g_ref, qd_ref, u_ref, do_ref, kk_ref):
    upper = triangle(True, f32)
    for group in units(heads, UNITS["c0"]):
        us = [u_ref[half(c), cols(h)] for c, h in group]
        dos = [do_ref[half(c), cols(h)] for c, h in group]
        dats = each(lambda do, u: (nt(u, do) * upper).astype(bf16), dos, us)
        dkus = [
            nn(dat, qd_ref[half(c), cols(h)]) * jnp.exp(-g_ref[half(c), cols(h)])
            for dat, (c, h) in zip(dats, group)
        ]
        for (c, h), dku in zip(group, dkus):
            kk_ref[half(c), cols(h)] = dku.astype(bf16)


def kernel_c2(
    heads, place, resets, k_ref, g_ref, b_ref, wb_ref, kt_ref, n_ref, e_ref, vp_ref, u_ref, du_ref, dt_ref,
    pq_ref, kk_ref, g0, g1, g2, g3, dk_ref, dv_ref, dd_ref, db_ref, state,
):
    step = pl.program_id(0)
    turn = pl.num_programs(0) - 1 - step

    @pl.when(step == 0)
    def _():
        collect(place[1], state, (g0, g1, g2, g3))

    weights = twice(True)
    ones = jnp.ones((16, 128), bf16)
    grads = {}
    gbs = {}
    now = [state[h] for h in range(heads)]
    for c in reversed(range(STEP)):
        keep = (turn * STEP + c != resets[0]).astype(f32)
        for h in range(heads):
            grads[c, h] = now[h]
            gbs[c, h] = now[h].astype(bf16)
        for h in range(heads):
            lam = jnp.exp(g_ref[64 * c + 63 : 64 * c + 64, cols(h)])
            now[h] = keep * (dt_ref[c, h].astype(f32) + lam * now[h] - nt(gbs[c, h], n_ref[c, h]))
    for h in range(heads):
        state[h] = now[h]
    for group in reversed(units(heads, UNITS["c2"])):
        gb = [gbs[p] for p in group]
        dus = [
            (du_ref[half(c), cols(h)].astype(f32) + nt(kt_ref[half(c), cols(h)], x)).astype(bf16)
            for x, (c, h) in zip(gb, group)
        ]
        dvs = [tn(wb_ref[c, :, half(h)], du) for du, (c, h) in zip(dus, group)]
        dvbs = each(lambda x: x.astype(bf16), dvs)
        gs = [g_ref[half(c), cols(h)] for c, h in group]
        ktts = [
            nn(u_ref[half(c), cols(h)], x) * jnp.exp(g[63:64, :] - g) for x, g, (c, h) in zip(gb, gs, group)
        ]
        kdds = [nn(dvb, e_ref[c, h]) * jnp.exp(g) for dvb, g, (c, h) in zip(dvbs, gs, group)]
        ks = [k_ref[half(c), cols(h)].astype(f32) for c, h in group]
        rks = each(inverse_norm, ks)
        kus = each(lambda k, rk: k * rk, ks, rks)
        sums = [kk_ref[half(c), cols(h)].astype(f32) + ktt for ktt, (c, h) in zip(ktts, group)]
        dkus = each(lambda x, kdd: x - kdd, sums, kdds)
        dks = each(
            lambda rk, dku, ku: (rk * (dku - ku * jnp.sum(ku * dku, axis=-1, keepdims=True))).astype(bf16),
            rks, dkus, kus,
        )
        kutts = each(lambda ku, ktt: ku * ktt, kus, ktts)
        dgams = [
            pq_ref[half(c), cols(h)] - ku * (x + kdd) for ku, kdd, x, (c, h) in zip(kus, kdds, sums, group)
        ]
        dlasts = [
            jnp.sum(kutt, axis=0, keepdims=True)
            + jnp.exp(g[63:64, :]) * jnp.sum(grads[c, h] * e_ref[c, h].astype(f32), axis=0, keepdims=True)
            for kutt, g, (c, h) in zip(kutts, gs, group)
        ]
        dds = each(lambda dgam, dlast: sum_rows(weights, dgam) + dlast, dgams, dlasts)
        dbs = [
            nt(ones, (dv * vp_ref[half(c), cols(h)].astype(f32)).astype(bf16))[0:1]
            for dv, (c, h) in zip(dvs, group)
        ]
        for (c, h), dvb, dk, dd, db in zip(group, dvbs, dks, dds, dbs):
            dv_ref[half(c), cols(h)] = dvb
            dk_ref[half(c), cols(h)] = dk
            dd_ref[half(c), cols(h)] = dd
            db_ref[h : h + 1, half(c)] = db / b_ref[h : h + 1, half(c)]


def identity_pair():
    row = lax.broadcasted_iota(jnp.int32, (256, 128), 0)
    col = lax.broadcasted_iota(jnp.int32, (256, 128), 1)
    return (row == col + 128).astype(bf16)


def after(pair, r):
    moved = nn(r, pair[128:256])
    return jnp.concatenate([moved[0:128] + pair[0:128].astype(f32), moved[128:256]], axis=0)


def kernel_f1(heads, place, p0, p1, p2, p3, total_ref, before_ref, slots):
    collect(place[1], slots, (p0, p1, p2, p3))
    before_ref[0] = identity_pair()
    r = slots[0]
    for z in range(1, RING):
        before_ref[z] = r
        r = after(slots[z], r).astype(bf16)
    total_ref[...] = r


def kernel_m(heads, slots, m_ref):
    row = lax.broadcasted_iota(jnp.int32, (128, 128), 0)
    col = lax.broadcasted_iota(jnp.int32, (128, 128), 1)
    m_ref[RING - 1] = (row == col).astype(bf16)
    m = slots[RING - 1, 128:256]
    m_ref[RING - 2] = m
    for z in reversed(range(1, RING - 1)):
        m = nn(slots[z, 128:256], m).astype(bf16)
        m_ref[z - 1] = m


def kernel_f2(heads, place, p0, p1, p2, p3, before, o0, o1, o2, o3, slots, states):
    me = place[0]
    collect(me, slots, (p0, p1, p2, p3))
    s = jnp.where(me > 0, slots[0, 0:128].astype(f32), 0.0)
    for i in range(1, RING - 1):
        moved = nn(s.astype(bf16), slots[i, 128:256]) + slots[i, 0:128].astype(f32)
        s = jnp.where(i < me, moved, s)
    sb = s.astype(bf16)
    moved = [nn(sb, before[z, 128:256]) for z in range(RING)]
    for z in range(RING):
        states[z] = (moved[z] + before[z, 0:128].astype(f32)).astype(bf16)
    spread(place[1], states, (o0, o1, o2, o3))


def kernel_r1(heads, place, p0, p1, p2, p3, before, total_ref, slots):
    collect(place[1], slots, (p0, p1, p2, p3))
    parts = [nt(slots[z], before[z, 128:256]) for z in range(1, RING)]
    total_ref[...] = (slots[0].astype(f32) + sum(parts)).astype(bf16)


def kernel_r3(heads, slots, zslots, later_ref):
    later_ref[RING - 1] = jnp.zeros((128, 128), bf16)
    g = slots[RING - 1]
    later_ref[RING - 2] = g
    for z in reversed(range(1, RING - 1)):
        g = (nt(g, zslots[z, 128:256]) + slots[z].astype(f32)).astype(bf16)
        later_ref[z - 1] = g


def kernel_r2(heads, place, p0, p1, p2, p3, later, later_m, yslots, o0, o1, o2, o3, slots, grads):
    me = place[0]
    collect(me, slots, (p0, p1, p2, p3))
    g = jnp.where(me < RING - 1, slots[RING - 1].astype(f32), 0.0)
    for i in reversed(range(1, RING - 1)):
        moved = nt(g.astype(bf16), yslots[i, 128:256]) + slots[i].astype(f32)
        g = jnp.where(i > me, moved, g)
    gb = g.astype(bf16)
    moved = [nt(gb, later_m[z]) for z in range(RING)]
    for z in range(RING):
        grads[z] = (moved[z] + later[z].astype(f32)).astype(bf16)
    spread(place[1], grads, (o0, o1, o2, o3))


def permute(x, distance, outer):
    size = lax.axis_size("seq")
    if outer:
        pairs = [(i, (i + RING * distance) % size) for i in range(size)]
    else:
        pairs = [(i, i // RING * RING + (i + distance) % RING) for i in range(size)]
    return lax.ppermute(x, "seq", pairs)


def three(x, outer):
    arrays = [x] * RING if outer else x
    return [arrays[0]] + [permute(arrays[distance], distance, outer) for distance in (1, 2, 3)]


BIG = 54 * 2**20
SMALL = 8 * 2**20
SMEM = pl.BlockSpec(memory_space=pltpu.SMEM)
VMEM = pl.BlockSpec(memory_space=pltpu.VMEM)


def shape(dims, dtype):
    return jax.ShapeDtypeStruct(dims, dtype)


def call(body, name, heads, in_specs, out_specs, out_shape, scratch, grid, flops, *args):
    total = sum(a.size * a.dtype.itemsize for a in args)
    total += sum(o.size * o.dtype.itemsize for o in out_shape)
    return pl.pallas_call(
        functools.partial(body, heads),
        out_shape=out_shape,
        grid=grid,
        in_specs=in_specs,
        out_specs=out_specs,
        scratch_shapes=scratch,
        compiler_params=pltpu.CompilerParams(
            vmem_limit_bytes=BIG if grid else SMALL,
            **({"dimension_semantics": ("arbitrary",)} if grid else {}),
        ),
        cost_estimate=pl.CostEstimate(flops=flops, bytes_accessed=total, transcendentals=0),
        name=name,
    )(*args)


def per_device(
    queries, keys, values, decay, beta, wy_inverse, out_gate, norm_gain, out_proj, grad_out, resets
):
    tokens = queries.shape[0]
    heads = beta.shape[0]
    count = tokens // GROUP
    steps = count // STEP
    width = heads * 128
    index = lax.axis_index("seq")
    place = jnp.stack([index // RING, index % RING]).astype(jnp.int32)
    gathered = lax.all_gather(grad_out, "head", axis=1, tiled=True)

    def specs(back):
        at = (lambda i: steps - 1 - i) if back else (lambda i: i)
        return dict(
            tok=pl.BlockSpec((STEP * GROUP, width), lambda i: (at(i), 0)),
            beta=pl.BlockSpec((heads, STEP * GROUP), lambda i: (0, at(i))),
            wy=pl.BlockSpec((STEP, GROUP, heads * GROUP), lambda i: (at(i), 0, 0)),
            state=pl.BlockSpec((STEP, heads, 128, 128), lambda i: (at(i), 0, 0, 0)),
            pair=pl.BlockSpec((STEP, heads, 256, 128), lambda i: (at(i), 0, 0, 0)),
            whole=pl.BlockSpec((128, 128), lambda i: (0, 0)),
            whole2=pl.BlockSpec((256, 128), lambda i: (0, 0)),
            gain=pl.BlockSpec((1, 128), lambda i: (0, 0)),
        )

    s = specs(False)
    tok_b = shape((tokens, width), bf16)
    tok_f = shape((tokens, width), f32)
    small_b = shape((count, GROUP, heads * GROUP), bf16)
    state_b = shape((count, heads, 128, 128), bf16)
    pair_b = shape((count, heads, 256, 128), bf16)
    one_b = shape((128, 128), bf16)
    two_b = shape((256, 128), bf16)
    ones_b = shape((RING, 128, 128), bf16)
    twos_b = shape((RING, 256, 128), bf16)
    unit = count * heads * 2 * 64 * 128 * 128

    gamma, wb, kd, kt, y, n, pre, *mb = call(
        kernel_a1, "a1", heads,
        [SMEM, SMEM, s["tok"], s["tok"], s["tok"], s["beta"], s["wy"]],
        [s["tok"], s["wy"], s["tok"], s["tok"], s["tok"], s["state"], s["pair"]] + [s["whole2"]] * 4,
        [tok_f, small_b, tok_b, tok_b, tok_b, state_b, pair_b] + [two_b] * 4,
        [pltpu.VMEM((heads, 256, 128), f32)], (steps,), 8 * unit,
        place, resets, keys, values, decay, beta, wy_inverse,
    )
    zs = three(mb, False)
    qd, ki, a, at = call(
        kernel_a2, "a2", heads,
        [s["tok"], s["tok"], s["tok"]],
        [s["tok"], s["tok"], s["wy"], s["wy"]],
        [tok_b, tok_b, small_b, small_b],
        [], (steps,), 2 * unit, queries, keys, gamma,
    )
    zs, qd = lax.optimization_barrier((zs, qd))
    group, before, zslots = call(
        kernel_f1, "f1", heads, [SMEM] + [VMEM] * 4, [VMEM] * 3, [two_b, twos_b, twos_b], [], (),
        unit // 8, place, *zs,
    )
    ys = three(group, True)
    (later_m,) = call(kernel_m, "m", heads, [VMEM], [VMEM], [ones_b], [], (), unit // 16, zslots)
    ys, later_m = lax.optimization_barrier((ys, later_m))
    *states, yslots = call(
        kernel_f2, "f2", heads, [SMEM] + [VMEM] * 5, [VMEM] * 5, [one_b] * 4 + [twos_b],
        [pltpu.VMEM((RING, 128, 128), bf16)], (), unit // 8, place, *ys, before,
    )
    state_in = three(states, False)
    upstream = lax.dot_general(
        gathered, out_proj, (((1,), (1,)), ((), ())), preferred_element_type=f32
    ).astype(bf16)
    state_in, upstream = lax.optimization_barrier((state_in, upstream))
    e, vp, u, do, du, dt, dgate, *r = call(
        kernel_b, "b", heads,
        [SMEM, s["tok"], s["tok"], s["tok"], s["tok"], s["wy"], s["wy"], s["wy"], s["pair"], s["tok"], s["tok"], s["gain"]] + [s["whole"]] * 4,
        [s["state"], s["tok"], s["tok"], s["tok"], s["tok"], s["state"], s["tok"]] + [s["whole"]] * 4,
        [state_b, tok_b, tok_b, tok_b, tok_b, state_b, tok_b] + [one_b] * 4,
        [pltpu.VMEM((heads, 128, 128), f32), pltpu.VMEM((heads, 128, 128), bf16)], (steps,), 12 * unit,
        place, values, kd, qd, y, wb, a, at, pre, out_gate, upstream, norm_gain.reshape(1, 128), *state_in,
    )
    zr = three(r, False)
    (kk,) = call(
        kernel_c0, "c0", heads, [s["tok"]] * 4, [s["tok"]], [tok_b], [], (steps,), 2 * unit, gamma, qd, u, do,
    )
    zr, kk = lax.optimization_barrier((zr, kk))
    rgroup, rslots = call(
        kernel_r1, "r1", heads, [SMEM] + [VMEM] * 5, [VMEM] * 2, [one_b, ones_b], [], (),
        unit // 16, place, *zr, before,
    )
    yr = three(rgroup, True)
    (later,) = call(kernel_r3, "r3", heads, [VMEM] * 2, [VMEM], [ones_b], [], (), unit // 16, rslots, zslots)
    dq, pq = call(
        kernel_c1, "c1", heads,
        [s["tok"]] * 5 + [s["state"]],
        [s["tok"], s["tok"]], [tok_b, tok_f],
        [], (steps,), 4 * unit, queries, gamma, ki, u, do, e,
    )
    yr, pq, later = lax.optimization_barrier((yr, pq, later))
    *grads, _ = call(
        kernel_r2, "r2", heads, [SMEM] + [VMEM] * 7, [VMEM] * 5, [one_b] * 4 + [ones_b],
        [pltpu.VMEM((RING, 128, 128), bf16)], (), unit // 16, place, *yr, later, later_m, yslots,
    )
    grad_in = three(grads, False)
    t = specs(True)
    dk, dv, dd, db = call(
        kernel_c2, "c2", heads,
        [SMEM, SMEM, t["tok"], t["tok"], t["beta"], t["wy"], t["tok"], t["state"], t["state"], t["tok"], t["tok"], t["tok"], t["state"], t["tok"], t["tok"]] + [t["whole"]] * 4,
        [t["tok"], t["tok"], t["tok"], t["beta"]],
        [tok_b, tok_b, tok_f, shape((heads, tokens), f32)],
        [pltpu.VMEM((heads, 128, 128), f32)], (steps,), 10 * unit,
        place, resets, keys, gamma, beta, wb, kt, n, e, vp, u, du, dt, pq, kk, *grad_in,
    )
    return dq, dk, dv, dd, db, dgate


def solution(mesh):
    return jax.shard_map(
        per_device,
        mesh=mesh,
        in_specs=(
            P("seq", "head"),
            P("seq", "head"),
            P("seq", "head"),
            P("seq", "head"),
            P("head", "seq"),
            P("seq", None, "head"),
            P("seq", "head"),
            P(),
            P("head", None),
            P("seq", "head"),
            P("seq"),
        ),
        out_specs=(
            P("seq", "head"),
            P("seq", "head"),
            P("seq", "head"),
            P("seq", "head"),
            P("head", "seq"),
            P("seq", "head"),
        ),
        check_vma=False,
    )
```

```python
import functools

import jax
import jax.numpy as jnp
from jax import lax
from jax.experimental import pallas as pl
from jax.experimental.pallas import tpu as pltpu
from jax.sharding import PartitionSpec as P

DK = 128
DV = 128
GROUP = 64
EPS = 1e-6
SCALE = DK**-0.5
STEP = dict(a1=4, a2=8, b=4, c0=8, c1=8, c2=4)
UNITS = dict(a1=16, a2=16, b=16, c0=16, c1=16, c2=16)
RING = 4

f32 = jnp.float32
bf16 = jnp.bfloat16


def nn(a, b):
    return lax.dot_general(a, b, (((1,), (0,)), ((), ())), preferred_element_type=f32)


def nt(a, b):
    return lax.dot_general(a, b, (((1,), (1,)), ((), ())), preferred_element_type=f32)


def tn(a, b):
    return lax.dot_general(a, b, (((0,), (0,)), ((), ())), preferred_element_type=f32)


def triangle(upper, dtype):
    row = lax.broadcasted_iota(jnp.int32, (GROUP, GROUP), 0)
    col = lax.broadcasted_iota(jnp.int32, (GROUP, GROUP), 1)
    return (row <= col if upper else row >= col).astype(dtype)


def sum_rows(weights, x):
    high = x.astype(bf16)
    low = (x - high.astype(f32)).astype(bf16)
    return nn(weights, jnp.concatenate([high, low], axis=0))


def twice(upper):
    t = triangle(upper, f32)
    return jnp.concatenate([t, t], axis=1).astype(bf16)


def inverse_norm(x):
    return lax.rsqrt(jnp.sum(x * x, axis=-1, keepdims=True) + EPS)


def cols(h):
    return slice(128 * h, 128 * h + 128)


def half(h):
    return slice(64 * h, 64 * h + 64)


def units(heads, name):
    size = UNITS[name]
    pairs = [(c, h) for c in range(STEP[name]) for h in range(heads)]
    return [pairs[i : i + size] for i in range(0, len(pairs), size)]


def each(f, *lists):
    return [f(*xs) for xs in zip(*lists)]


def spread(me, array, outs):
    for shift, out in enumerate(outs):
        out[...] = array[lax.rem(me + shift, RING)].astype(out.dtype)


def collect(me, array, arrived):
    for shift, other in enumerate(arrived):
        array[lax.rem(me + RING - shift, RING)] = other[...].astype(array.dtype)


def diag(x, y):
    zx = jnp.zeros((x.shape[0], y.shape[1]), x.dtype)
    zy = jnp.zeros((y.shape[0], x.shape[1]), x.dtype)
    return jnp.concatenate([jnp.concatenate([x, zx], axis=1), jnp.concatenate([zy, y], axis=1)], axis=0)


def lanes(x, y):
    return jnp.concatenate([x, y], axis=1)


def split(pairs):
    return [part for p in pairs for part in (p[:, 0:128], p[:, 128:256])]


def kernel_a1(
    heads, place, resets, k_ref, v_ref, d_ref, b_ref, w_ref,
    g_ref, wb_ref, kd_ref, kt_ref, y_ref, n_ref, pre_ref, o0, o1, o2, o3, state,
):
    step = pl.program_id(0)

    @pl.when(step == 0)
    def _():
        row = lax.broadcasted_iota(jnp.int32, (256, 128), 0)
        col = lax.broadcasted_iota(jnp.int32, (256, 128), 1)
        for h in range(heads):
            state[h] = (row == col + 128).astype(f32)

    weights = twice(False)
    gammas = [sum_rows(weights, d_ref[half(c), :]) for c in range(STEP["a1"])]
    for c in range(STEP["a1"]):
        g_ref[half(c), :] = gammas[c]
    rs = [state[h] for h in range(heads)]
    for group in units(heads, "a1"):
        gs = [gammas[c][:, cols(h)] for c, h in group]
        ks = [k_ref[half(c), cols(h)].astype(f32) for c, h in group]
        kus = each(lambda k: k * inverse_norm(k), ks)
        kds = each(lambda ku, g: (ku * jnp.exp(g)).astype(bf16), kus, gs)
        kts = each(lambda ku, g: (ku * jnp.exp(g[63:64, :] - g)).astype(bf16), kus, gs)
        wbs = [(w_ref[c, :, half(h)] * b_ref[h : h + 1, half(c)]).astype(bf16) for c, h in group]
        xys = [
            nn(wb, jnp.concatenate([v_ref[half(c), cols(h)], kd], axis=1)).astype(bf16)
            for wb, kd, (c, h) in zip(wbs, kds, group)
        ]
        bns = each(tn, xys, kts)
        ns = each(lambda bn: bn[128:].astype(bf16), bns)
        for (c, h), wb, kd, kt, xy, n in zip(group, wbs, kds, kts, xys, ns):
            wb_ref[c, :, half(h)] = wb
            kd_ref[half(c), cols(h)] = kd
            kt_ref[half(c), cols(h)] = kt
            y_ref[half(c), cols(h)] = xy[:, 128:]
            n_ref[c, h] = n
        for (c, h), bn, n, g in zip(group, bns, ns, gs):
            keep = (step * STEP["a1"] + c != resets[0]).astype(f32)
            r = rs[h] * keep
            rb = r.astype(bf16)
            pre_ref[c, h] = rb
            r = jnp.exp(g[63:64, :]) * r - nn(rb, n)
            rs[h] = jnp.concatenate([r[0:128] + bn[0:128], r[128:256]], axis=0)
    for h in range(heads):
        state[h] = rs[h]

    @pl.when(step == pl.num_programs(0) - 1)
    def _():
        spread(place[1], state, (o0, o1, o2, o3))


def kernel_a2(heads, q_ref, k_ref, g_ref, qd_ref, ki_ref, a_ref, at_ref):
    lower = triangle(False, f32)
    upper = triangle(True, f32)
    for group in units(heads, "a2"):
        gs = [g_ref[half(c), cols(h)] for c, h in group]
        qs = [q_ref[half(c), cols(h)].astype(f32) for c, h in group]
        ks = [k_ref[half(c), cols(h)].astype(f32) for c, h in group]
        qds = each(lambda q, g: (q * (inverse_norm(q) * SCALE) * jnp.exp(g)).astype(bf16), qs, gs)
        kis = each(lambda k, g: (k * inverse_norm(k) * jnp.exp(-g)).astype(bf16), ks, gs)
        als = each(lambda qd, ki: (nt(qd, ki) * lower).astype(bf16), qds, kis)
        ats = each(lambda qd, ki: (nt(ki, qd) * upper).astype(bf16), qds, kis)
        for (c, h), qd, ki, a, at in zip(group, qds, kis, als, ats):
            qd_ref[half(c), cols(h)] = qd
            ki_ref[half(c), cols(h)] = ki
            a_ref[c, :, half(h)] = a
            at_ref[c, :, half(h)] = at


def kernel_b(
    heads, place, v_ref, kd_ref, qd_ref, y_ref, wb_ref, a_ref, at_ref, pre_ref, gate_ref, x_ref, p_ref, gain_ref,
    s0, s1, s2, s3, e_ref, vp_ref, u_ref, do_ref, du_ref, dt_ref, dg_ref, r0, r1, r2, r3, total, s_ref,
):
    step = pl.program_id(0)

    @pl.when(step == 0)
    def _():
        total[...] = jnp.zeros_like(total)
        collect(place[1], s_ref, (s0, s1, s2, s3))

    gain = gain_ref[...]
    sums = [total[h] for h in range(heads)]
    up = nn(p_ref[...], x_ref[...]).astype(bf16).T
    for group in units(heads, "b"):
        es = split([
            nn(lanes(s_ref[h], s_ref[h + 1]), diag(pre_ref[c, h, 128:256], pre_ref[c, h + 1, 128:256]))
            for c, h in group[::2]
        ])
        es = [(pre_ref[c, h, 0:128].astype(f32) + e).astype(bf16) for e, (c, h) in zip(es, group)]
        boths = split([
            nt(
                jnp.concatenate([kd_ref[half(c), 128 * h : 128 * h + 256], qd_ref[half(c), 128 * h : 128 * h + 256]], axis=0),
                diag(es[i], es[i + 1]),
            )
            for i, (c, h) in list(enumerate(group))[::2]
        ])
        vps = [
            (v_ref[half(c), cols(h)].astype(f32) - both[0:64]).astype(bf16)
            for both, (c, h) in zip(boths, group)
        ]
        us = split([
            nn(wb_ref[c, :, 64 * h : 64 * h + 128], diag(vps[i], vps[i + 1])).astype(bf16)
            for i, (c, h) in list(enumerate(group))[::2]
        ])
        os = split([
            nn(a_ref[c, :, 64 * h : 64 * h + 128], diag(us[i], us[i + 1]))
            for i, (c, h) in list(enumerate(group))[::2]
        ])
        os = each(lambda both, o: both[64:128] + o, boths, os)
        rmss = each(lambda o: lax.rsqrt(jnp.mean(o * o, axis=-1, keepdims=True) + EPS), os)
        sigs = [jax.nn.sigmoid(gate_ref[half(c), cols(h)].astype(f32)) for c, h in group]
        ws = [up[half(c), cols(h)].astype(f32) * gain * sig for sig, (c, h) in zip(sigs, group)]
        ons = each(lambda o, rms: o * rms, os, rmss)
        wons = each(lambda w, on: w * on, ws, ons)
        dgs = each(lambda won, sig: (won * (1.0 - sig)).astype(bf16), wons, sigs)
        dos = each(
            lambda rms, w, on, won: (rms * (w - on * jnp.mean(won, axis=-1, keepdims=True))).astype(bf16),
            rmss, ws, ons, wons,
        )
        dus = split([
            nn(at_ref[c, :, 64 * h : 64 * h + 128], diag(dos[i], dos[i + 1])).astype(bf16)
            for i, (c, h) in list(enumerate(group))[::2]
        ])
        dts = split([
            tn(
                jnp.concatenate([dos[i], dus[i], dos[i + 1], dus[i + 1]], axis=0),
                diag(
                    jnp.concatenate([qd_ref[half(c), cols(h)], -y_ref[half(c), cols(h)]], axis=0),
                    jnp.concatenate([qd_ref[half(c), cols(h + 1)], -y_ref[half(c), cols(h + 1)]], axis=0),
                ),
            ).astype(bf16)
            for i, (c, h) in list(enumerate(group))[::2]
        ])
        for h in range(heads):
            mine = [(dt, c) for dt, (c, x) in zip(dts, group) if x == h]
            for (d0, c0), (d1, c1) in zip(mine[::2], mine[1::2]):
                sums[h] = sums[h] + nt(lanes(d0, d1), lanes(pre_ref[c0, h, 128:256], pre_ref[c1, h, 128:256]))
        for (c, h), e, vp, u, do, du, dt, dg in zip(group, es, vps, us, dos, dus, dts, dgs):
            e_ref[c, h] = e
            vp_ref[half(c), cols(h)] = vp
            u_ref[half(c), cols(h)] = u
            do_ref[half(c), cols(h)] = do
            du_ref[half(c), cols(h)] = du
            dt_ref[c, h] = dt
            dg_ref[half(c), cols(h)] = dg
    for h in range(heads):
        total[h] = sums[h]

    @pl.when(step == pl.num_programs(0) - 1)
    def _():
        spread(place[1], total, (r0, r1, r2, r3))


def kernel_c1(heads, q_ref, g_ref, ki_ref, u_ref, do_ref, e_ref, dq_ref, pq_ref):
    lower = triangle(False, f32)
    for group in units(heads, "c1"):
        us = [u_ref[half(c), cols(h)] for c, h in group]
        dos = [do_ref[half(c), cols(h)] for c, h in group]
        das = each(lambda do, u: (nt(do, u) * lower).astype(bf16), dos, us)
        dqus = [
            (nn(do, e_ref[c, h]) + nn(da, ki_ref[half(c), cols(h)])) * jnp.exp(g_ref[half(c), cols(h)])
            for do, da, (c, h) in zip(dos, das, group)
        ]
        qs = [q_ref[half(c), cols(h)].astype(f32) for c, h in group]
        rqs = each(lambda q: inverse_norm(q), qs)
        qns = each(lambda q, rq: q * rq, qs, rqs)
        prods = each(lambda qn, dqu: qn * dqu, qns, dqus)
        dqs = each(
            lambda rq, dqu, qn, prod: (
                (rq * SCALE) * (dqu - qn * jnp.sum(prod, axis=-1, keepdims=True))
            ).astype(bf16),
            rqs, dqus, qns, prods,
        )
        for (c, h), dq, prod in zip(group, dqs, prods):
            dq_ref[half(c), cols(h)] = dq
            pq_ref[half(c), cols(h)] = prod * SCALE


def kernel_c0(heads, g_ref, qd_ref, u_ref, do_ref, kk_ref):
    upper = triangle(True, f32)
    for group in units(heads, "c0"):
        us = [u_ref[half(c), cols(h)] for c, h in group]
        dos = [do_ref[half(c), cols(h)] for c, h in group]
        dats = each(lambda do, u: (nt(u, do) * upper).astype(bf16), dos, us)
        dkus = [
            nn(dat, qd_ref[half(c), cols(h)]) * jnp.exp(-g_ref[half(c), cols(h)])
            for dat, (c, h) in zip(dats, group)
        ]
        for (c, h), dku in zip(group, dkus):
            kk_ref[half(c), cols(h)] = dku.astype(bf16)


def kernel_c2(
    heads, place, resets, k_ref, g_ref, b_ref, wb_ref, kt_ref, n_ref, e_ref, vp_ref, u_ref, du_ref, dt_ref,
    pq_ref, kk_ref, g0, g1, g2, g3, dk_ref, dv_ref, dd_ref, db_ref, state,
):
    step = pl.program_id(0)
    turn = pl.num_programs(0) - 1 - step

    @pl.when(step == 0)
    def _():
        collect(place[1], state, (g0, g1, g2, g3))

    weights = twice(True)
    ones = jnp.ones((16, 128), bf16)
    grads = {}
    gbs = {}
    now = [state[h] for h in range(heads)]
    for c in reversed(range(STEP["c2"])):
        keep = (turn * STEP["c2"] + c != resets[0]).astype(f32)
        for h in range(heads):
            grads[c, h] = now[h]
            gbs[c, h] = now[h].astype(bf16)
        for h in range(heads):
            lam = jnp.exp(g_ref[64 * c + 63 : 64 * c + 64, cols(h)])
            now[h] = keep * (dt_ref[c, h].astype(f32) + lam * now[h] - nt(gbs[c, h], n_ref[c, h]))
    for h in range(heads):
        state[h] = now[h]
    for group in reversed(units(heads, "c2")):
        gb = [gbs[p] for p in group]
        dus = [
            (du_ref[half(c), cols(h)].astype(f32) + nt(kt_ref[half(c), cols(h)], x)).astype(bf16)
            for x, (c, h) in zip(gb, group)
        ]
        dvs = [tn(wb_ref[c, :, half(h)], du) for du, (c, h) in zip(dus, group)]
        dvbs = each(lambda x: x.astype(bf16), dvs)
        gs = [g_ref[half(c), cols(h)] for c, h in group]
        ktts = [
            nn(u_ref[half(c), cols(h)], x) * jnp.exp(g[63:64, :] - g) for x, g, (c, h) in zip(gb, gs, group)
        ]
        kdds = [nn(dvb, e_ref[c, h]) * jnp.exp(g) for dvb, g, (c, h) in zip(dvbs, gs, group)]
        ks = [k_ref[half(c), cols(h)].astype(f32) for c, h in group]
        rks = each(inverse_norm, ks)
        kus = each(lambda k, rk: k * rk, ks, rks)
        sums = [kk_ref[half(c), cols(h)].astype(f32) + ktt for ktt, (c, h) in zip(ktts, group)]
        dkus = each(lambda x, kdd: x - kdd, sums, kdds)
        dks = each(
            lambda rk, dku, ku: (rk * (dku - ku * jnp.sum(ku * dku, axis=-1, keepdims=True))).astype(bf16),
            rks, dkus, kus,
        )
        kutts = each(lambda ku, ktt: ku * ktt, kus, ktts)
        dgams = [
            pq_ref[half(c), cols(h)] - ku * (x + kdd) for ku, kdd, x, (c, h) in zip(kus, kdds, sums, group)
        ]
        dlasts = [
            jnp.sum(kutt, axis=0, keepdims=True)
            + jnp.exp(g[63:64, :]) * jnp.sum(grads[c, h] * e_ref[c, h].astype(f32), axis=0, keepdims=True)
            for kutt, g, (c, h) in zip(kutts, gs, group)
        ]
        dds = each(lambda dgam, dlast: sum_rows(weights, dgam) + dlast, dgams, dlasts)
        dbs = [
            nt(ones, (dv * vp_ref[half(c), cols(h)].astype(f32)).astype(bf16))[0:1]
            for dv, (c, h) in zip(dvs, group)
        ]
        for (c, h), dvb, dk, dd, db in zip(group, dvbs, dks, dds, dbs):
            dv_ref[half(c), cols(h)] = dvb
            dk_ref[half(c), cols(h)] = dk
            dd_ref[half(c), cols(h)] = dd
            db_ref[h : h + 1, half(c)] = db / b_ref[h : h + 1, half(c)]


def identity_pair():
    row = lax.broadcasted_iota(jnp.int32, (256, 128), 0)
    col = lax.broadcasted_iota(jnp.int32, (256, 128), 1)
    return (row == col + 128).astype(bf16)


def after(pair, r):
    moved = nn(r, pair[128:256])
    return jnp.concatenate([moved[0:128] + pair[0:128].astype(f32), moved[128:256]], axis=0)


def kernel_f1(heads, place, p0, p1, p2, p3, total_ref, before_ref, slots):
    collect(place[1], slots, (p0, p1, p2, p3))
    before_ref[0] = identity_pair()
    r = slots[0]
    for z in range(1, RING):
        before_ref[z] = r
        r = after(slots[z], r).astype(bf16)
    total_ref[...] = r


def kernel_m(heads, slots, m_ref):
    row = lax.broadcasted_iota(jnp.int32, (128, 128), 0)
    col = lax.broadcasted_iota(jnp.int32, (128, 128), 1)
    m_ref[RING - 1] = (row == col).astype(bf16)
    m = slots[RING - 1, 128:256]
    m_ref[RING - 2] = m
    for z in reversed(range(1, RING - 1)):
        m = nn(slots[z, 128:256], m).astype(bf16)
        m_ref[z - 1] = m


def kernel_f2(heads, place, p0, p1, p2, p3, before, o0, o1, o2, o3, slots, states):
    me = place[0]
    collect(me, slots, (p0, p1, p2, p3))
    s = jnp.where(me > 0, slots[0, 0:128].astype(f32), 0.0)
    for i in range(1, RING - 1):
        moved = nn(s.astype(bf16), slots[i, 128:256]) + slots[i, 0:128].astype(f32)
        s = jnp.where(i < me, moved, s)
    sb = s.astype(bf16)
    moved = [nn(sb, before[z, 128:256]) for z in range(RING)]
    for z in range(RING):
        states[z] = (moved[z] + before[z, 0:128].astype(f32)).astype(bf16)
    spread(place[1], states, (o0, o1, o2, o3))


def kernel_r1(heads, place, p0, p1, p2, p3, before, total_ref, slots):
    collect(place[1], slots, (p0, p1, p2, p3))
    parts = [nt(slots[z], before[z, 128:256]) for z in range(1, RING)]
    total_ref[...] = (slots[0].astype(f32) + sum(parts)).astype(bf16)


def kernel_r3(heads, slots, zslots, later_ref):
    later_ref[RING - 1] = jnp.zeros((128, 128), bf16)
    g = slots[RING - 1]
    later_ref[RING - 2] = g
    for z in reversed(range(1, RING - 1)):
        g = (nt(g, zslots[z, 128:256]) + slots[z].astype(f32)).astype(bf16)
        later_ref[z - 1] = g


def kernel_r2(heads, place, p0, p1, p2, p3, later, later_m, yslots, o0, o1, o2, o3, slots, grads):
    me = place[0]
    collect(me, slots, (p0, p1, p2, p3))
    g = jnp.where(me < RING - 1, slots[RING - 1].astype(f32), 0.0)
    for i in reversed(range(1, RING - 1)):
        moved = nt(g.astype(bf16), yslots[i, 128:256]) + slots[i].astype(f32)
        g = jnp.where(i > me, moved, g)
    gb = g.astype(bf16)
    moved = [nt(gb, later_m[z]) for z in range(RING)]
    for z in range(RING):
        grads[z] = (moved[z] + later[z].astype(f32)).astype(bf16)
    spread(place[1], grads, (o0, o1, o2, o3))


def permute(x, distance, outer):
    size = lax.axis_size("seq")
    if outer:
        pairs = [(i, (i + RING * distance) % size) for i in range(size)]
    else:
        pairs = [(i, i // RING * RING + (i + distance) % RING) for i in range(size)]
    return lax.ppermute(x, "seq", pairs)


def three(x, outer):
    arrays = [x] * RING if outer else x
    return [arrays[0]] + [permute(arrays[distance], distance, outer) for distance in (1, 2, 3)]


LIMIT = dict(a1=54, a2=54, b=53, c0=54, c1=54, c2=53)
SMEM = pl.BlockSpec(memory_space=pltpu.SMEM)
VMEM = pl.BlockSpec(memory_space=pltpu.VMEM)


def shape(dims, dtype):
    return jax.ShapeDtypeStruct(dims, dtype)


def call(body, name, heads, in_specs, out_specs, out_shape, scratch, grid, flops, *args):
    total = sum(a.size * a.dtype.itemsize for a in args)
    total += sum(o.size * o.dtype.itemsize for o in out_shape)
    return pl.pallas_call(
        functools.partial(body, heads),
        out_shape=out_shape,
        grid=grid,
        in_specs=in_specs,
        out_specs=out_specs,
        scratch_shapes=scratch,
        compiler_params=pltpu.CompilerParams(
            vmem_limit_bytes=LIMIT.get(name, 8) * 2**20,
            **({"dimension_semantics": ("arbitrary",)} if grid else {}),
        ),
        cost_estimate=pl.CostEstimate(flops=flops, bytes_accessed=total, transcendentals=0),
        name=name,
    )(*args)


def per_device(
    queries, keys, values, decay, beta, wy_inverse, out_gate, norm_gain, out_proj, grad_out, resets
):
    tokens = queries.shape[0]
    heads = beta.shape[0]
    count = tokens // GROUP
    width = heads * 128
    index = lax.axis_index("seq")
    place = jnp.stack([index // RING, index % RING]).astype(jnp.int32)
    gathered = lax.all_gather(grad_out.T, "head", axis=0, tiled=True)
    model = out_proj.shape[1]

    def specs(name, back=False):
        step = STEP[name]
        steps = count // step
        at = (lambda i: steps - 1 - i) if back else (lambda i: i)
        return dict(
            grid=(steps,),
            tok=pl.BlockSpec((step * GROUP, width), lambda i: (at(i), 0)),
            beta=pl.BlockSpec((heads, step * GROUP), lambda i: (0, at(i))),
            wy=pl.BlockSpec((step, GROUP, heads * GROUP), lambda i: (at(i), 0, 0)),
            state=pl.BlockSpec((step, heads, 128, 128), lambda i: (at(i), 0, 0, 0)),
            pair=pl.BlockSpec((step, heads, 256, 128), lambda i: (at(i), 0, 0, 0)),
            whole=pl.BlockSpec((128, 128), lambda i: (0, 0)),
            whole2=pl.BlockSpec((256, 128), lambda i: (0, 0)),
            parts=pl.BlockSpec((model, step * GROUP), lambda i: (0, at(i))),
            proj=pl.BlockSpec((width, model), lambda i: (0, 0)),
            gain=pl.BlockSpec((1, 128), lambda i: (0, 0)),
        )

    tok_b = shape((tokens, width), bf16)
    tok_f = shape((tokens, width), f32)
    small_b = shape((count, GROUP, heads * GROUP), bf16)
    state_b = shape((count, heads, 128, 128), bf16)
    pair_b = shape((count, heads, 256, 128), bf16)
    one_b = shape((128, 128), bf16)
    two_b = shape((256, 128), bf16)
    ones_b = shape((RING, 128, 128), bf16)
    twos_b = shape((RING, 256, 128), bf16)
    unit = count * heads * 2 * 64 * 128 * 128

    s = specs("a1")
    gamma, wb, kd, kt, y, n, pre, *mb = call(
        kernel_a1, "a1", heads,
        [SMEM, SMEM, s["tok"], s["tok"], s["tok"], s["beta"], s["wy"]],
        [s["tok"], s["wy"], s["tok"], s["tok"], s["tok"], s["state"], s["pair"]] + [s["whole2"]] * 4,
        [tok_f, small_b, tok_b, tok_b, tok_b, state_b, pair_b] + [two_b] * 4,
        [pltpu.VMEM((heads, 256, 128), f32)], s["grid"], 8 * unit,
        place, resets, keys, values, decay, beta, wy_inverse,
    )
    zs = three(mb, False)
    s = specs("a2")
    qd, ki, a, at = call(
        kernel_a2, "a2", heads,
        [s["tok"], s["tok"], s["tok"]],
        [s["tok"], s["tok"], s["wy"], s["wy"]],
        [tok_b, tok_b, small_b, small_b],
        [], s["grid"], 2 * unit, queries, keys, gamma,
    )
    zs, qd = lax.optimization_barrier((zs, qd))
    group, before, zslots = call(
        kernel_f1, "f1", heads, [SMEM] + [VMEM] * 4, [VMEM] * 3, [two_b, twos_b, twos_b], [], (),
        unit // 8, place, *zs,
    )
    ys = three(group, True)
    (later_m,) = call(kernel_m, "m", heads, [VMEM], [VMEM], [ones_b], [], (), unit // 16, zslots)
    ys, later_m = lax.optimization_barrier((ys, later_m))
    *states, yslots = call(
        kernel_f2, "f2", heads, [SMEM] + [VMEM] * 5, [VMEM] * 5, [one_b] * 4 + [twos_b],
        [pltpu.VMEM((RING, 128, 128), bf16)], (), unit // 8, place, *ys, before,
    )
    state_in = three(states, False)
    s = specs("b")
    e, vp, u, do, du, dt, dgate, *r = call(
        kernel_b, "b", heads,
        [SMEM, s["tok"], s["tok"], s["tok"], s["tok"], s["wy"], s["wy"], s["wy"], s["pair"], s["tok"], s["parts"], s["proj"], s["gain"]] + [s["whole"]] * 4,
        [s["state"], s["tok"], s["tok"], s["tok"], s["tok"], s["state"], s["tok"]] + [s["whole"]] * 4,
        [state_b, tok_b, tok_b, tok_b, tok_b, state_b, tok_b] + [one_b] * 4,
        [pltpu.VMEM((heads, 128, 128), f32), pltpu.VMEM((heads, 128, 128), bf16)], s["grid"], 12 * unit,
        place, values, kd, qd, y, wb, a, at, pre, out_gate, gathered, out_proj, norm_gain.reshape(1, 128), *state_in,
    )
    zr = three(r, False)
    s = specs("c0")
    (kk,) = call(
        kernel_c0, "c0", heads, [s["tok"]] * 4, [s["tok"]], [tok_b], [], s["grid"], 2 * unit, gamma, qd, u, do,
    )
    zr, kk = lax.optimization_barrier((zr, kk))
    rgroup, rslots = call(
        kernel_r1, "r1", heads, [SMEM] + [VMEM] * 5, [VMEM] * 2, [one_b, ones_b], [], (),
        unit // 16, place, *zr, before,
    )
    yr = three(rgroup, True)
    (later,) = call(kernel_r3, "r3", heads, [VMEM] * 2, [VMEM], [ones_b], [], (), unit // 16, rslots, zslots)
    yr, later = lax.optimization_barrier((yr, later))
    *grads, _ = call(
        kernel_r2, "r2", heads, [SMEM] + [VMEM] * 7, [VMEM] * 5, [one_b] * 4 + [ones_b],
        [pltpu.VMEM((RING, 128, 128), bf16)], (), unit // 16, place, *yr, later, later_m, yslots,
    )
    grad_in = three(grads, False)
    s = specs("c1")
    dq, pq = call(
        kernel_c1, "c1", heads,
        [s["tok"]] * 5 + [s["state"]],
        [s["tok"], s["tok"]], [tok_b, tok_f],
        [], s["grid"], 4 * unit, queries, gamma, ki, u, do, e,
    )
    grad_in, pq = lax.optimization_barrier((grad_in, pq))
    s = specs("c2", True)
    dk, dv, dd, db = call(
        kernel_c2, "c2", heads,
        [SMEM, SMEM, s["tok"], s["tok"], s["beta"], s["wy"], s["tok"], s["state"], s["state"], s["tok"], s["tok"], s["tok"], s["state"], s["tok"], s["tok"]] + [s["whole"]] * 4,
        [s["tok"], s["tok"], s["tok"], s["beta"]],
        [tok_b, tok_b, tok_f, shape((heads, tokens), f32)],
        [pltpu.VMEM((heads, 128, 128), f32)], s["grid"], 10 * unit,
        place, resets, keys, gamma, beta, wb, kt, n, e, vp, u, du, dt, pq, kk, *grad_in,
    )
    return dq, dk, dv, dd, db, dgate


def solution(mesh):
    return jax.shard_map(
        per_device,
        mesh=mesh,
        in_specs=(
            P("seq", "head"),
            P("seq", "head"),
            P("seq", "head"),
            P("seq", "head"),
            P("head", "seq"),
            P("seq", None, "head"),
            P("seq", "head"),
            P(),
            P("head", None),
            P("seq", "head"),
            P("seq"),
        ),
        out_specs=(
            P("seq", "head"),
            P("seq", "head"),
            P("seq", "head"),
            P("seq", "head"),
            P("head", "seq"),
            P("seq", "head"),
        ),
        check_vma=False,
    )
```

```python
import functools

import jax
import jax.numpy as jnp
from jax import lax
from jax.experimental import pallas as pl
from jax.experimental.pallas import tpu as pltpu
from jax.sharding import PartitionSpec as P

DK = 128
DV = 128
GROUP = 64
EPS = 1e-6
SCALE = DK**-0.5
STEP = dict(a1=4, a2=8, b=4, c0=8, c1=4, c2=4)
UNITS = dict(a1=16, a2=16, b=16, c0=16, c1=16, c2=16)
RING = 4

f32 = jnp.float32
bf16 = jnp.bfloat16


def nn(a, b):
    return lax.dot_general(a, b, (((1,), (0,)), ((), ())), preferred_element_type=f32)


def nt(a, b):
    return lax.dot_general(a, b, (((1,), (1,)), ((), ())), preferred_element_type=f32)


def tn(a, b):
    return lax.dot_general(a, b, (((0,), (0,)), ((), ())), preferred_element_type=f32)


def triangle(upper, dtype):
    row = lax.broadcasted_iota(jnp.int32, (GROUP, GROUP), 0)
    col = lax.broadcasted_iota(jnp.int32, (GROUP, GROUP), 1)
    return (row <= col if upper else row >= col).astype(dtype)


def sum_rows(weights, x):
    high = x.astype(bf16)
    low = (x - high.astype(f32)).astype(bf16)
    return nn(weights, jnp.concatenate([high, low], axis=0))


def twice(upper):
    t = triangle(upper, f32)
    return jnp.concatenate([t, t], axis=1).astype(bf16)


def inverse_norm(x):
    return lax.rsqrt(jnp.sum(x * x, axis=-1, keepdims=True) + EPS)


def cols(h):
    return slice(128 * h, 128 * h + 128)


def half(h):
    return slice(64 * h, 64 * h + 64)


def units(heads, name):
    size = UNITS[name]
    pairs = [(c, h) for c in range(STEP[name]) for h in range(heads)]
    return [pairs[i : i + size] for i in range(0, len(pairs), size)]


def each(f, *lists):
    return [f(*xs) for xs in zip(*lists)]


def outer():
    return lax.axis_index("seq") // RING


def inner():
    return lax.rem(lax.axis_index("seq"), RING)


def spread(me, array, outs):
    for shift, out in enumerate(outs):
        out[...] = array[lax.rem(me + shift, RING)].astype(out.dtype)


def collect(me, array, arrived):
    for shift, other in enumerate(arrived):
        array[lax.rem(me + RING - shift, RING)] = other[...].astype(array.dtype)


def diag(x, y):
    zx = jnp.zeros((x.shape[0], y.shape[1]), x.dtype)
    zy = jnp.zeros((y.shape[0], x.shape[1]), x.dtype)
    return jnp.concatenate([jnp.concatenate([x, zx], axis=1), jnp.concatenate([zy, y], axis=1)], axis=0)


def lanes(x, y):
    return jnp.concatenate([x, y], axis=1)


def split(pairs):
    return [part for p in pairs for part in (p[:, 0:128], p[:, 128:256])]


def kernel_a1(
    heads, resets, k_ref, v_ref, d_ref, b_ref, w_ref,
    g_ref, wb_ref, kd_ref, kt_ref, y_ref, n_ref, pre_ref, o0, o1, o2, o3, state,
):
    step = pl.program_id(0)

    @pl.when(step == 0)
    def _():
        row = lax.broadcasted_iota(jnp.int32, (256, 128), 0)
        col = lax.broadcasted_iota(jnp.int32, (256, 128), 1)
        for h in range(heads):
            state[h] = (row == col + 128).astype(f32)

    weights = twice(False)
    gammas = [sum_rows(weights, d_ref[half(c), :]) for c in range(STEP["a1"])]
    for c in range(STEP["a1"]):
        g_ref[half(c), :] = gammas[c]
    rs = [state[h] for h in range(heads)]
    for group in units(heads, "a1"):
        gs = [gammas[c][:, cols(h)] for c, h in group]
        ks = [k_ref[half(c), cols(h)].astype(f32) for c, h in group]
        kus = each(lambda k: k * inverse_norm(k), ks)
        kds = each(lambda ku, g: (ku * jnp.exp(g)).astype(bf16), kus, gs)
        kts = each(lambda ku, g: (ku * jnp.exp(g[63:64, :] - g)).astype(bf16), kus, gs)
        wbs = [(w_ref[c, :, half(h)] * b_ref[h : h + 1, half(c)]).astype(bf16) for c, h in group]
        xys = [
            nn(wb, jnp.concatenate([v_ref[half(c), cols(h)], kd], axis=1)).astype(bf16)
            for wb, kd, (c, h) in zip(wbs, kds, group)
        ]
        bns = each(tn, xys, kts)
        ns = each(lambda bn: bn[128:].astype(bf16), bns)
        for (c, h), wb, kd, kt, xy, n in zip(group, wbs, kds, kts, xys, ns):
            wb_ref[c, :, half(h)] = wb
            kd_ref[half(c), cols(h)] = kd
            kt_ref[half(c), cols(h)] = kt
            y_ref[half(c), cols(h)] = xy[:, 128:]
            n_ref[c, h] = n
        for (c, h), bn, n, g in zip(group, bns, ns, gs):
            keep = (step * STEP["a1"] + c != resets[0]).astype(f32)
            r = rs[h] * keep
            rb = r.astype(bf16)
            pre_ref[c, h] = rb
            r = jnp.exp(g[63:64, :]) * r - nn(rb, n)
            rs[h] = jnp.concatenate([r[0:128] + bn[0:128], r[128:256]], axis=0)
    for h in range(heads):
        state[h] = rs[h]

    @pl.when(step == pl.num_programs(0) - 1)
    def _():
        spread(inner(), state, (o0, o1, o2, o3))


def kernel_a2(heads, q_ref, k_ref, g_ref, qd_ref, ki_ref, a_ref, at_ref):
    lower = triangle(False, f32)
    upper = triangle(True, f32)
    for group in units(heads, "a2"):
        gs = [g_ref[half(c), cols(h)] for c, h in group]
        qs = [q_ref[half(c), cols(h)].astype(f32) for c, h in group]
        ks = [k_ref[half(c), cols(h)].astype(f32) for c, h in group]
        qds = each(lambda q, g: (q * (inverse_norm(q) * SCALE) * jnp.exp(g)).astype(bf16), qs, gs)
        kis = each(lambda k, g: (k * inverse_norm(k) * jnp.exp(-g)).astype(bf16), ks, gs)
        als = each(lambda qd, ki: (nt(qd, ki) * lower).astype(bf16), qds, kis)
        ats = each(lambda qd, ki: (nt(ki, qd) * upper).astype(bf16), qds, kis)
        for (c, h), qd, ki, a, at in zip(group, qds, kis, als, ats):
            qd_ref[half(c), cols(h)] = qd
            ki_ref[half(c), cols(h)] = ki
            a_ref[c, :, half(h)] = a
            at_ref[c, :, half(h)] = at


def kernel_b(
    heads, v_ref, kd_ref, qd_ref, y_ref, wb_ref, a_ref, at_ref, pre_ref, gate_ref, x_ref, p_ref, gain_ref,
    s0, s1, s2, s3, e_ref, vp_ref, u_ref, do_ref, du_ref, dt_ref, dg_ref, r0, r1, r2, r3, total, s_ref,
):
    step = pl.program_id(0)

    @pl.when(step == 0)
    def _():
        total[...] = jnp.zeros_like(total)
        collect(inner(), s_ref, (s0, s1, s2, s3))

    gain = gain_ref[...]
    sums = [total[h] for h in range(heads)]
    up = nn(p_ref[...], x_ref[...]).astype(bf16).T
    for group in units(heads, "b"):
        es = split([
            nn(lanes(s_ref[h], s_ref[h + 1]), diag(pre_ref[c, h, 128:256], pre_ref[c, h + 1, 128:256]))
            for c, h in group[::2]
        ])
        es = [(pre_ref[c, h, 0:128].astype(f32) + e).astype(bf16) for e, (c, h) in zip(es, group)]
        boths = split([
            nt(
                jnp.concatenate([kd_ref[half(c), 128 * h : 128 * h + 256], qd_ref[half(c), 128 * h : 128 * h + 256]], axis=0),
                diag(es[i], es[i + 1]),
            )
            for i, (c, h) in list(enumerate(group))[::2]
        ])
        vps = [
            (v_ref[half(c), cols(h)].astype(f32) - both[0:64]).astype(bf16)
            for both, (c, h) in zip(boths, group)
        ]
        us = split([
            nn(wb_ref[c, :, 64 * h : 64 * h + 128], diag(vps[i], vps[i + 1])).astype(bf16)
            for i, (c, h) in list(enumerate(group))[::2]
        ])
        os = split([
            nn(a_ref[c, :, 64 * h : 64 * h + 128], diag(us[i], us[i + 1]))
            for i, (c, h) in list(enumerate(group))[::2]
        ])
        os = each(lambda both, o: both[64:128] + o, boths, os)
        rmss = each(lambda o: lax.rsqrt(jnp.mean(o * o, axis=-1, keepdims=True) + EPS), os)
        sigs = [jax.nn.sigmoid(gate_ref[half(c), cols(h)].astype(f32)) for c, h in group]
        ws = [up[half(c), cols(h)].astype(f32) * gain * sig for sig, (c, h) in zip(sigs, group)]
        ons = each(lambda o, rms: o * rms, os, rmss)
        wons = each(lambda w, on: w * on, ws, ons)
        dgs = each(lambda won, sig: (won * (1.0 - sig)).astype(bf16), wons, sigs)
        dos = each(
            lambda rms, w, on, won: (rms * (w - on * jnp.mean(won, axis=-1, keepdims=True))).astype(bf16),
            rmss, ws, ons, wons,
        )
        dus = split([
            nn(at_ref[c, :, 64 * h : 64 * h + 128], diag(dos[i], dos[i + 1])).astype(bf16)
            for i, (c, h) in list(enumerate(group))[::2]
        ])
        dts = split([
            tn(
                jnp.concatenate([dos[i], dus[i], dos[i + 1], dus[i + 1]], axis=0),
                diag(
                    jnp.concatenate([qd_ref[half(c), cols(h)], -y_ref[half(c), cols(h)]], axis=0),
                    jnp.concatenate([qd_ref[half(c), cols(h + 1)], -y_ref[half(c), cols(h + 1)]], axis=0),
                ),
            ).astype(bf16)
            for i, (c, h) in list(enumerate(group))[::2]
        ])
        for h in range(heads):
            mine = [(dt, c) for dt, (c, x) in zip(dts, group) if x == h]
            for (d0, c0), (d1, c1) in zip(mine[::2], mine[1::2]):
                sums[h] = sums[h] + nt(lanes(d0, d1), lanes(pre_ref[c0, h, 128:256], pre_ref[c1, h, 128:256]))
        for (c, h), e, vp, u, do, du, dt, dg in zip(group, es, vps, us, dos, dus, dts, dgs):
            e_ref[c, h] = e
            vp_ref[half(c), cols(h)] = vp
            u_ref[half(c), cols(h)] = u
            do_ref[half(c), cols(h)] = do
            du_ref[half(c), cols(h)] = du
            dt_ref[c, h] = dt
            dg_ref[half(c), cols(h)] = dg
    for h in range(heads):
        total[h] = sums[h]

    @pl.when(step == pl.num_programs(0) - 1)
    def _():
        spread(inner(), total, (r0, r1, r2, r3))


def kernel_c1(heads, q_ref, g_ref, ki_ref, u_ref, do_ref, e_ref, *outs):
    dq_ref, pq_ref = outs[-2:]
    lower = triangle(False, f32)
    for group in units(heads, "c1"):
        us = [u_ref[half(c), cols(h)] for c, h in group]
        dos = [do_ref[half(c), cols(h)] for c, h in group]
        das = each(lambda do, u: (nt(do, u) * lower).astype(bf16), dos, us)
        dqus = [
            (nn(do, e_ref[c, h]) + nn(da, ki_ref[half(c), cols(h)])) * jnp.exp(g_ref[half(c), cols(h)])
            for do, da, (c, h) in zip(dos, das, group)
        ]
        qs = [q_ref[half(c), cols(h)].astype(f32) for c, h in group]
        rqs = each(lambda q: inverse_norm(q), qs)
        qns = each(lambda q, rq: q * rq, qs, rqs)
        prods = each(lambda qn, dqu: qn * dqu, qns, dqus)
        dqs = each(
            lambda rq, dqu, qn, prod: (
                (rq * SCALE) * (dqu - qn * jnp.sum(prod, axis=-1, keepdims=True))
            ).astype(bf16),
            rqs, dqus, qns, prods,
        )
        for (c, h), dq, prod in zip(group, dqs, prods):
            dq_ref[half(c), cols(h)] = dq
            pq_ref[half(c), cols(h)] = prod * SCALE


def kernel_c0(heads, g_ref, qd_ref, u_ref, do_ref, kk_ref):
    upper = triangle(True, f32)
    for group in units(heads, "c0"):
        us = [u_ref[half(c), cols(h)] for c, h in group]
        dos = [do_ref[half(c), cols(h)] for c, h in group]
        dats = each(lambda do, u: (nt(u, do) * upper).astype(bf16), dos, us)
        dkus = [
            nn(dat, qd_ref[half(c), cols(h)]) * jnp.exp(-g_ref[half(c), cols(h)])
            for dat, (c, h) in zip(dats, group)
        ]
        for (c, h), dku in zip(group, dkus):
            kk_ref[half(c), cols(h)] = dku.astype(bf16)


def kernel_c2(
    heads, resets, k_ref, g_ref, b_ref, wb_ref, kt_ref, n_ref, e_ref, vp_ref, u_ref, du_ref, dt_ref,
    pq_ref, kk_ref, g0, g1, g2, g3, dk_ref, dv_ref, dd_ref, db_ref, state,
):
    step = pl.program_id(0)
    turn = pl.num_programs(0) - 1 - step

    @pl.when(step == 0)
    def _():
        collect(inner(), state, (g0, g1, g2, g3))

    weights = twice(True)
    ones = jnp.ones((16, 128), bf16)
    grads = {}
    gbs = {}
    now = [state[h] for h in range(heads)]
    for c in reversed(range(STEP["c2"])):
        keep = (turn * STEP["c2"] + c != resets[0]).astype(f32)
        for h in range(heads):
            grads[c, h] = now[h]
            gbs[c, h] = now[h].astype(bf16)
        for h in range(heads):
            lam = jnp.exp(g_ref[64 * c + 63 : 64 * c + 64, cols(h)])
            now[h] = keep * (dt_ref[c, h].astype(f32) + lam * now[h] - nt(gbs[c, h], n_ref[c, h]))
    for h in range(heads):
        state[h] = now[h]
    for group in reversed(units(heads, "c2")):
        gb = [gbs[p] for p in group]
        dus = [
            (du_ref[half(c), cols(h)].astype(f32) + nt(kt_ref[half(c), cols(h)], x)).astype(bf16)
            for x, (c, h) in zip(gb, group)
        ]
        dvs = [tn(wb_ref[c, :, half(h)], du) for du, (c, h) in zip(dus, group)]
        dvbs = each(lambda x: x.astype(bf16), dvs)
        gs = [g_ref[half(c), cols(h)] for c, h in group]
        ktts = [
            nn(u_ref[half(c), cols(h)], x) * jnp.exp(g[63:64, :] - g) for x, g, (c, h) in zip(gb, gs, group)
        ]
        kdds = [nn(dvb, e_ref[c, h]) * jnp.exp(g) for dvb, g, (c, h) in zip(dvbs, gs, group)]
        ks = [k_ref[half(c), cols(h)].astype(f32) for c, h in group]
        rks = each(inverse_norm, ks)
        kus = each(lambda k, rk: k * rk, ks, rks)
        sums = [kk_ref[half(c), cols(h)].astype(f32) + ktt for ktt, (c, h) in zip(ktts, group)]
        dkus = each(lambda x, kdd: x - kdd, sums, kdds)
        dks = each(
            lambda rk, dku, ku: (rk * (dku - ku * jnp.sum(ku * dku, axis=-1, keepdims=True))).astype(bf16),
            rks, dkus, kus,
        )
        kutts = each(lambda ku, ktt: ku * ktt, kus, ktts)
        dgams = [
            pq_ref[half(c), cols(h)] - ku * (x + kdd) for ku, kdd, x, (c, h) in zip(kus, kdds, sums, group)
        ]
        dlasts = [
            jnp.sum(kutt, axis=0, keepdims=True)
            + jnp.exp(g[63:64, :]) * jnp.sum(grads[c, h] * e_ref[c, h].astype(f32), axis=0, keepdims=True)
            for kutt, g, (c, h) in zip(kutts, gs, group)
        ]
        dds = each(lambda dgam, dlast: sum_rows(weights, dgam) + dlast, dgams, dlasts)
        dbs = [
            nt(ones, (dv * vp_ref[half(c), cols(h)].astype(f32)).astype(bf16))[0:1]
            for dv, (c, h) in zip(dvs, group)
        ]
        for (c, h), dvb, dk, dd, db in zip(group, dvbs, dks, dds, dbs):
            dv_ref[half(c), cols(h)] = dvb
            dk_ref[half(c), cols(h)] = dk
            dd_ref[half(c), cols(h)] = dd
            db_ref[h : h + 1, half(c)] = db / b_ref[h : h + 1, half(c)]


def identity_pair():
    row = lax.broadcasted_iota(jnp.int32, (256, 128), 0)
    col = lax.broadcasted_iota(jnp.int32, (256, 128), 1)
    return (row == col + 128).astype(bf16)


def after(pair, r):
    moved = nn(r, pair[128:256])
    return jnp.concatenate([moved[0:128] + pair[0:128].astype(f32), moved[128:256]], axis=0)


def kernel_f1(heads, p0, p1, p2, p3, total_ref, before_ref, slots):
    collect(inner(), slots, (p0, p1, p2, p3))
    before_ref[0] = identity_pair()
    r = slots[0]
    for z in range(1, RING):
        before_ref[z] = r
        r = after(slots[z], r).astype(bf16)
    total_ref[...] = r


def kernel_m(heads, slots, m_ref):
    row = lax.broadcasted_iota(jnp.int32, (128, 128), 0)
    col = lax.broadcasted_iota(jnp.int32, (128, 128), 1)
    m_ref[RING - 1] = (row == col).astype(bf16)
    m = slots[RING - 1, 128:256]
    m_ref[RING - 2] = m
    for z in reversed(range(1, RING - 1)):
        m = nn(slots[z, 128:256], m).astype(bf16)
        m_ref[z - 1] = m


def kernel_f2(heads, p0, p1, p2, p3, before, o0, o1, o2, o3, slots, states):
    me = outer()
    collect(me, slots, (p0, p1, p2, p3))
    s = jnp.where(me > 0, slots[0, 0:128].astype(f32), 0.0)
    for i in range(1, RING - 1):
        moved = nn(s.astype(bf16), slots[i, 128:256]) + slots[i, 0:128].astype(f32)
        s = jnp.where(i < me, moved, s)
    sb = s.astype(bf16)
    moved = [nn(sb, before[z, 128:256]) for z in range(RING)]
    for z in range(RING):
        states[z] = (moved[z] + before[z, 0:128].astype(f32)).astype(bf16)
    spread(inner(), states, (o0, o1, o2, o3))


def kernel_r1(heads, p0, p1, p2, p3, before, total_ref, slots):
    collect(inner(), slots, (p0, p1, p2, p3))
    parts = [nt(slots[z], before[z, 128:256]) for z in range(1, RING)]
    total_ref[...] = (slots[0].astype(f32) + sum(parts)).astype(bf16)


def kernel_r3(heads, slots, zslots, later_ref):
    later_ref[RING - 1] = jnp.zeros((128, 128), bf16)
    g = slots[RING - 1]
    later_ref[RING - 2] = g
    for z in reversed(range(1, RING - 1)):
        g = (nt(g, zslots[z, 128:256]) + slots[z].astype(f32)).astype(bf16)
        later_ref[z - 1] = g


def kernel_r2(heads, p0, p1, p2, p3, later, later_m, yslots, o0, o1, o2, o3, slots, grads):
    me = outer()
    collect(me, slots, (p0, p1, p2, p3))
    g = jnp.where(me < RING - 1, slots[RING - 1].astype(f32), 0.0)
    for i in reversed(range(1, RING - 1)):
        moved = nt(g.astype(bf16), yslots[i, 128:256]) + slots[i].astype(f32)
        g = jnp.where(i > me, moved, g)
    gb = g.astype(bf16)
    moved = [nt(gb, later_m[z]) for z in range(RING)]
    for z in range(RING):
        grads[z] = (moved[z] + later[z].astype(f32)).astype(bf16)
    spread(inner(), grads, (o0, o1, o2, o3))


def permute(x, distance, outer):
    size = lax.axis_size("seq")
    if outer:
        pairs = [(i, (i + RING * distance) % size) for i in range(size)]
    else:
        pairs = [(i, i // RING * RING + (i + distance) % RING) for i in range(size)]
    return lax.ppermute(x, "seq", pairs)


def three(x, outer):
    arrays = [x] * RING if outer else x
    return [arrays[0]] + [permute(arrays[distance], distance, outer) for distance in (1, 2, 3)]


LIMIT = dict(a1=54, a2=54, b=53, c0=54, c1=54, c2=53)
SMEM = pl.BlockSpec(memory_space=pltpu.SMEM)
VMEM = pl.BlockSpec(memory_space=pltpu.VMEM)


def shape(dims, dtype):
    return jax.ShapeDtypeStruct(dims, dtype)


def call(body, name, heads, in_specs, out_specs, out_shape, scratch, grid, flops, *args, into=()):
    total = sum(a.size * a.dtype.itemsize for a in args)
    total += sum(o.size * o.dtype.itemsize for o in out_shape)
    return pl.pallas_call(
        functools.partial(body, heads),
        out_shape=out_shape,
        grid=grid,
        in_specs=in_specs,
        out_specs=out_specs,
        scratch_shapes=scratch,
        input_output_aliases={len(args) + i: i for i in range(len(into))},
        compiler_params=pltpu.CompilerParams(
            vmem_limit_bytes=LIMIT.get(name, 8) * 2**20,
            **({"dimension_semantics": ("arbitrary",)} if grid else {}),
        ),
        cost_estimate=pl.CostEstimate(flops=flops, bytes_accessed=total, transcendentals=0),
        name=name,
    )(*args, *into)


def per_device(
    queries, keys, values, decay, beta, wy_inverse, out_gate, norm_gain, out_proj, grad_out, resets
):
    tokens = queries.shape[0]
    heads = beta.shape[0]
    count = tokens // GROUP
    width = heads * 128
    gathered = lax.all_gather(grad_out.T, "head", axis=0, tiled=True)
    model = out_proj.shape[1]

    def specs(name, back=False):
        step = STEP[name]
        steps = count // step
        at = (lambda i: steps - 1 - i) if back else (lambda i: i)
        return dict(
            grid=(steps,),
            tok=pl.BlockSpec((step * GROUP, width), lambda i: (at(i), 0)),
            beta=pl.BlockSpec((heads, step * GROUP), lambda i: (0, at(i))),
            wy=pl.BlockSpec((step, GROUP, heads * GROUP), lambda i: (at(i), 0, 0)),
            state=pl.BlockSpec((step, heads, 128, 128), lambda i: (at(i), 0, 0, 0)),
            pair=pl.BlockSpec((step, heads, 256, 128), lambda i: (at(i), 0, 0, 0)),
            whole=pl.BlockSpec((128, 128), lambda i: (0, 0)),
            whole2=pl.BlockSpec((256, 128), lambda i: (0, 0)),
            parts=pl.BlockSpec((model, step * GROUP), lambda i: (0, at(i))),
            proj=pl.BlockSpec((width, model), lambda i: (0, 0)),
            gain=pl.BlockSpec((1, 128), lambda i: (0, 0)),
        )

    tok_b = shape((tokens, width), bf16)
    tok_f = shape((tokens, width), f32)
    small_b = shape((count, GROUP, heads * GROUP), bf16)
    state_b = shape((count, heads, 128, 128), bf16)
    pair_b = shape((count, heads, 256, 128), bf16)
    one_b = shape((128, 128), bf16)
    two_b = shape((256, 128), bf16)
    ones_b = shape((RING, 128, 128), bf16)
    twos_b = shape((RING, 256, 128), bf16)
    unit = count * heads * 2 * 64 * 128 * 128

    s = specs("a1")
    gamma, wb, kd, kt, y, n, pre, *mb = call(
        kernel_a1, "a1", heads,
        [SMEM, s["tok"], s["tok"], s["tok"], s["beta"], s["wy"]],
        [s["tok"], s["wy"], s["tok"], s["tok"], s["tok"], s["state"], s["pair"]] + [s["whole2"]] * 4,
        [tok_f, small_b, tok_b, tok_b, tok_b, state_b, pair_b] + [two_b] * 4,
        [pltpu.VMEM((heads, 256, 128), f32)], s["grid"], 8 * unit,
        resets, keys, values, decay, beta, wy_inverse,
    )
    zs = three(mb, False)
    s = specs("a2")
    qd, ki, a, at = call(
        kernel_a2, "a2", heads,
        [s["tok"], s["tok"], s["tok"]],
        [s["tok"], s["tok"], s["wy"], s["wy"]],
        [tok_b, tok_b, small_b, small_b],
        [], s["grid"], 2 * unit, queries, keys, gamma,
    )
    zs, qd = lax.optimization_barrier((zs, qd))
    group, before, zslots = call(
        kernel_f1, "f1", heads, [VMEM] * 4, [VMEM] * 3, [two_b, twos_b, twos_b], [], (),
        unit // 8, *zs,
    )
    ys = three(group, True)
    (later_m,) = call(kernel_m, "m", heads, [VMEM], [VMEM], [ones_b], [], (), unit // 16, zslots)
    ys, later_m = lax.optimization_barrier((ys, later_m))
    *states, yslots = call(
        kernel_f2, "f2", heads, [VMEM] * 5, [VMEM] * 5, [one_b] * 4 + [twos_b],
        [pltpu.VMEM((RING, 128, 128), bf16)], (), unit // 8, *ys, before,
    )
    state_in = three(states, False)
    s = specs("b")
    e, vp, u, do, du, dt, dgate, *r = call(
        kernel_b, "b", heads,
        [s["tok"], s["tok"], s["tok"], s["tok"], s["wy"], s["wy"], s["wy"], s["pair"], s["tok"], s["parts"], s["proj"], s["gain"]] + [s["whole"]] * 4,
        [s["state"], s["tok"], s["tok"], s["tok"], s["tok"], s["state"], s["tok"]] + [s["whole"]] * 4,
        [state_b, tok_b, tok_b, tok_b, tok_b, state_b, tok_b] + [one_b] * 4,
        [pltpu.VMEM((heads, 128, 128), f32), pltpu.VMEM((heads, 128, 128), bf16)], s["grid"], 12 * unit,
        values, kd, qd, y, wb, a, at, pre, out_gate, gathered, out_proj, norm_gain.reshape(1, 128), *state_in,
    )
    zr = three(r, False)
    s = specs("c0")
    (kk,) = call(
        kernel_c0, "c0", heads, [s["tok"]] * 4, [s["tok"]], [tok_b], [], s["grid"], 2 * unit, gamma, qd, u, do,
    )
    zr, kk = lax.optimization_barrier((zr, kk))
    rgroup, rslots = call(
        kernel_r1, "r1", heads, [VMEM] * 5, [VMEM] * 2, [one_b, ones_b], [], (),
        unit // 16, *zr, before,
    )
    yr = three(rgroup, True)
    (later,) = call(kernel_r3, "r3", heads, [VMEM] * 2, [VMEM], [ones_b], [], (), unit // 16, rslots, zslots)

    def gradient_q(part, into):
        steps = count // STEP["c1"] // 2
        tok = pl.BlockSpec((STEP["c1"] * GROUP, width), lambda i: (i + part * steps, 0))
        state = pl.BlockSpec((STEP["c1"], heads, 128, 128), lambda i: (i + part * steps, 0, 0, 0))
        return call(
            kernel_c1, "c1", heads,
            [tok] * 5 + [state] + [pl.BlockSpec(memory_space=pl.ANY)] * len(into),
            [tok, tok], [tok_b, tok_f],
            [], (steps,), 2 * unit, queries, gamma, ki, u, do, e, into=into,
        )

    dq, pq = gradient_q(0, ())
    yr, later, pq = lax.optimization_barrier((yr, later, pq))
    *grads, _ = call(
        kernel_r2, "r2", heads, [VMEM] * 7, [VMEM] * 5, [one_b] * 4 + [ones_b],
        [pltpu.VMEM((RING, 128, 128), bf16)], (), unit // 16, *yr, later, later_m, yslots,
    )
    grad_in = three(grads, False)
    dq, pq = gradient_q(1, (dq, pq))
    grad_in, pq = lax.optimization_barrier((grad_in, pq))
    s = specs("c2", True)
    dk, dv, dd, db = call(
        kernel_c2, "c2", heads,
        [SMEM, s["tok"], s["tok"], s["beta"], s["wy"], s["tok"], s["state"], s["state"], s["tok"], s["tok"], s["tok"], s["state"], s["tok"], s["tok"]] + [s["whole"]] * 4,
        [s["tok"], s["tok"], s["tok"], s["beta"]],
        [tok_b, tok_b, tok_f, shape((heads, tokens), f32)],
        [pltpu.VMEM((heads, 128, 128), f32)], s["grid"], 10 * unit,
        resets, keys, gamma, beta, wb, kt, n, e, vp, u, du, dt, pq, kk, *grad_in,
    )
    return dq, dk, dv, dd, db, dgate


def solution(mesh):
    return jax.shard_map(
        per_device,
        mesh=mesh,
        in_specs=(
            P("seq", "head"),
            P("seq", "head"),
            P("seq", "head"),
            P("seq", "head"),
            P("head", "seq"),
            P("seq", None, "head"),
            P("seq", "head"),
            P(),
            P("head", None),
            P("seq", "head"),
            P("seq"),
        ),
        out_specs=(
            P("seq", "head"),
            P("seq", "head"),
            P("seq", "head"),
            P("seq", "head"),
            P("head", "seq"),
            P("seq", "head"),
        ),
        check_vma=False,
    )
```

```python
import functools

import jax
import jax.numpy as jnp
from jax import lax
from jax.experimental import pallas as pl
from jax.experimental.pallas import tpu as pltpu
from jax.sharding import PartitionSpec as P

DK = 128
DV = 128
GROUP = 64
EPS = 1e-6
SCALE = DK**-0.5
STEP = dict(a1=4, a2=8, b=4, c0=8, c1=4, c2=4)
UNITS = dict(a1=16, a2=16, b=16, c0=16, c1=16, c2=16)
RING = 4

f32 = jnp.float32
bf16 = jnp.bfloat16


def nn(a, b):
    return lax.dot_general(a, b, (((1,), (0,)), ((), ())), preferred_element_type=f32)


def nt(a, b):
    return lax.dot_general(a, b, (((1,), (1,)), ((), ())), preferred_element_type=f32)


def tn(a, b):
    return lax.dot_general(a, b, (((0,), (0,)), ((), ())), preferred_element_type=f32)


def triangle(upper, dtype):
    row = lax.broadcasted_iota(jnp.int32, (GROUP, GROUP), 0)
    col = lax.broadcasted_iota(jnp.int32, (GROUP, GROUP), 1)
    return (row <= col if upper else row >= col).astype(dtype)


def sum_rows(weights, x):
    high = x.astype(bf16)
    low = (x - high.astype(f32)).astype(bf16)
    return nn(weights, jnp.concatenate([high, low], axis=0))


def twice(upper):
    t = triangle(upper, f32)
    return jnp.concatenate([t, t], axis=1).astype(bf16)


def inverse_norm(x):
    return lax.rsqrt(jnp.sum(x * x, axis=-1, keepdims=True) + EPS)


def cols(h):
    return slice(128 * h, 128 * h + 128)


def wide(h):
    return slice(128 * h, 128 * h + 256)


def half(h):
    return slice(64 * h, 64 * h + 64)


def units(heads, name):
    size = UNITS[name]
    pairs = [(c, h) for c in range(STEP[name]) for h in range(heads)]
    return [pairs[i : i + size] for i in range(0, len(pairs), size)]


def each(f, *lists):
    return [f(*xs) for xs in zip(*lists)]


def outer():
    return lax.axis_index("seq") // RING


def inner():
    return lax.rem(lax.axis_index("seq"), RING)


def spread(me, array, outs):
    for shift, out in enumerate(outs):
        out[...] = array[lax.rem(me + shift, RING)].astype(out.dtype)


def collect(me, array, arrived):
    for shift, other in enumerate(arrived):
        array[lax.rem(me + RING - shift, RING)] = other[...].astype(array.dtype)


def diag(x, y):
    zx = jnp.zeros((x.shape[0], y.shape[1]), x.dtype)
    zy = jnp.zeros((y.shape[0], x.shape[1]), x.dtype)
    return jnp.concatenate([jnp.concatenate([x, zx], axis=1), jnp.concatenate([zy, y], axis=1)], axis=0)


def lanes(x, y):
    return jnp.concatenate([x, y], axis=1)


def split(pairs):
    return [part for p in pairs for part in (p[:, 0:128], p[:, 128:256])]


def kernel_a1(
    heads, resets, k_ref, v_ref, d_ref, b_ref, w_ref,
    g_ref, wb_ref, kd_ref, kt_ref, y_ref, n_ref, pre_ref, o0, o1, o2, o3, state,
):
    step = pl.program_id(0)

    @pl.when(step == 0)
    def _():
        row = lax.broadcasted_iota(jnp.int32, (256, 128), 0)
        col = lax.broadcasted_iota(jnp.int32, (256, 128), 1)
        for h in range(heads):
            state[h] = (row == col + 128).astype(f32)

    weights = twice(False)
    gammas = [sum_rows(weights, d_ref[half(c), :]) for c in range(STEP["a1"])]
    for c in range(STEP["a1"]):
        g_ref[half(c), :] = gammas[c]
    rs = [state[h] for h in range(heads)]
    for group in units(heads, "a1"):
        gs = [gammas[c][:, cols(h)] for c, h in group]
        ks = [k_ref[half(c), cols(h)].astype(f32) for c, h in group]
        kus = each(lambda k: k * inverse_norm(k), ks)
        kds = each(lambda ku, g: (ku * jnp.exp(g)).astype(bf16), kus, gs)
        kts = each(lambda ku, g: (ku * jnp.exp(g[63:64, :] - g)).astype(bf16), kus, gs)
        wbs = [(w_ref[c, :, half(h)] * b_ref[h : h + 1, half(c)]).astype(bf16) for c, h in group]
        xys = [
            nn(wb, jnp.concatenate([v_ref[half(c), cols(h)], kd], axis=1)).astype(bf16)
            for wb, kd, (c, h) in zip(wbs, kds, group)
        ]
        bns = each(tn, xys, kts)
        ns = each(lambda bn: bn[128:].astype(bf16), bns)
        for (c, h), wb, kd, kt, xy, n in zip(group, wbs, kds, kts, xys, ns):
            wb_ref[c, :, half(h)] = wb
            kd_ref[half(c), cols(h)] = kd
            kt_ref[half(c), cols(h)] = kt
            y_ref[half(c), cols(h)] = xy[:, 128:]
            n_ref[c, h] = n
        for (c, h), bn, n, g in zip(group, bns, ns, gs):
            keep = (step * STEP["a1"] + c != resets[0]).astype(f32)
            r = rs[h] * keep
            rb = r.astype(bf16)
            pre_ref[c, h] = rb
            r = jnp.exp(g[63:64, :]) * r - nn(rb, n)
            rs[h] = jnp.concatenate([r[0:128] + bn[0:128], r[128:256]], axis=0)
    for h in range(heads):
        state[h] = rs[h]

    @pl.when(step == pl.num_programs(0) - 1)
    def _():
        spread(inner(), state, (o0, o1, o2, o3))


def kernel_a2(heads, q_ref, k_ref, g_ref, qd_ref, ki_ref, a_ref, at_ref):
    lower = triangle(False, f32)
    upper = triangle(True, f32)
    for group in units(heads, "a2"):
        gs = [g_ref[half(c), cols(h)] for c, h in group]
        qs = [q_ref[half(c), cols(h)].astype(f32) for c, h in group]
        ks = [k_ref[half(c), cols(h)].astype(f32) for c, h in group]
        qds = each(lambda q, g: (q * (inverse_norm(q) * SCALE) * jnp.exp(g)).astype(bf16), qs, gs)
        kis = each(lambda k, g: (k * inverse_norm(k) * jnp.exp(-g)).astype(bf16), ks, gs)
        als = each(lambda qd, ki: (nt(qd, ki) * lower).astype(bf16), qds, kis)
        ats = each(lambda qd, ki: (nt(ki, qd) * upper).astype(bf16), qds, kis)
        for (c, h), qd, ki, a, at in zip(group, qds, kis, als, ats):
            qd_ref[half(c), cols(h)] = qd
            ki_ref[half(c), cols(h)] = ki
            a_ref[c, :, half(h)] = a
            at_ref[c, :, half(h)] = at


def kernel_b(
    heads, v_ref, kd_ref, qd_ref, y_ref, wb_ref, a_ref, at_ref, pre_ref, gate_ref, x_ref, p_ref, gain_ref,
    s0, s1, s2, s3, e_ref, vp_ref, u_ref, do_ref, du_ref, dt_ref, dg_ref, r0, r1, r2, r3, total, s_ref,
):
    step = pl.program_id(0)

    @pl.when(step == 0)
    def _():
        total[...] = jnp.zeros_like(total)
        collect(inner(), s_ref, (s0, s1, s2, s3))

    gain = gain_ref[...]
    sums = [total[h] for h in range(heads)]
    up = nn(p_ref[...], x_ref[...]).astype(bf16).T
    for group in units(heads, "b"):
        es = split([
            nn(lanes(s_ref[h], s_ref[h + 1]), diag(pre_ref[c, h, 128:256], pre_ref[c, h + 1, 128:256]))
            for c, h in group[::2]
        ])
        es = [(pre_ref[c, h, 0:128].astype(f32) + e).astype(bf16) for e, (c, h) in zip(es, group)]
        boths = split([
            nt(
                jnp.concatenate([kd_ref[half(c), 128 * h : 128 * h + 256], qd_ref[half(c), 128 * h : 128 * h + 256]], axis=0),
                diag(es[i], es[i + 1]),
            )
            for i, (c, h) in list(enumerate(group))[::2]
        ])
        vps = [
            (v_ref[half(c), cols(h)].astype(f32) - both[0:64]).astype(bf16)
            for both, (c, h) in zip(boths, group)
        ]
        us = split([
            nn(wb_ref[c, :, 64 * h : 64 * h + 128], diag(vps[i], vps[i + 1])).astype(bf16)
            for i, (c, h) in list(enumerate(group))[::2]
        ])
        os = split([
            nn(a_ref[c, :, 64 * h : 64 * h + 128], diag(us[i], us[i + 1]))
            for i, (c, h) in list(enumerate(group))[::2]
        ])
        os = each(lambda both, o: both[64:128] + o, boths, os)
        rmss = each(lambda o: lax.rsqrt(jnp.mean(o * o, axis=-1, keepdims=True) + EPS), os)
        sigs = [jax.nn.sigmoid(gate_ref[half(c), cols(h)].astype(f32)) for c, h in group]
        ws = [up[half(c), cols(h)].astype(f32) * gain * sig for sig, (c, h) in zip(sigs, group)]
        ons = each(lambda o, rms: o * rms, os, rmss)
        wons = each(lambda w, on: w * on, ws, ons)
        dgs = each(lambda won, sig: (won * (1.0 - sig)).astype(bf16), wons, sigs)
        dos = each(
            lambda rms, w, on, won: (rms * (w - on * jnp.mean(won, axis=-1, keepdims=True))).astype(bf16),
            rmss, ws, ons, wons,
        )
        dus = split([
            nn(at_ref[c, :, 64 * h : 64 * h + 128], diag(dos[i], dos[i + 1])).astype(bf16)
            for i, (c, h) in list(enumerate(group))[::2]
        ])
        dts = split([
            tn(
                jnp.concatenate([dos[i], dus[i], dos[i + 1], dus[i + 1]], axis=0),
                diag(
                    jnp.concatenate([qd_ref[half(c), cols(h)], -y_ref[half(c), cols(h)]], axis=0),
                    jnp.concatenate([qd_ref[half(c), cols(h + 1)], -y_ref[half(c), cols(h + 1)]], axis=0),
                ),
            ).astype(bf16)
            for i, (c, h) in list(enumerate(group))[::2]
        ])
        for h in range(heads):
            mine = [(dt, c) for dt, (c, x) in zip(dts, group) if x == h]
            for (d0, c0), (d1, c1) in zip(mine[::2], mine[1::2]):
                sums[h] = sums[h] + nt(lanes(d0, d1), lanes(pre_ref[c0, h, 128:256], pre_ref[c1, h, 128:256]))
        for (c, h), e, vp, u, do, du, dt, dg in zip(group, es, vps, us, dos, dus, dts, dgs):
            e_ref[c, h] = e
            vp_ref[half(c), cols(h)] = vp
            u_ref[half(c), cols(h)] = u
            do_ref[half(c), cols(h)] = do
            du_ref[half(c), cols(h)] = du
            dt_ref[c, h] = dt
            dg_ref[half(c), cols(h)] = dg
    for h in range(heads):
        total[h] = sums[h]

    @pl.when(step == pl.num_programs(0) - 1)
    def _():
        spread(inner(), total, (r0, r1, r2, r3))


def kernel_c1(heads, q_ref, g_ref, ki_ref, u_ref, do_ref, e_ref, *outs):
    dq_ref, pq_ref = outs[-2:]
    lower = triangle(False, f32)
    for group in units(heads, "c1"):
        us = [u_ref[half(c), cols(h)] for c, h in group]
        dos = [do_ref[half(c), cols(h)] for c, h in group]
        das = each(lambda do, u: (nt(do, u) * lower).astype(bf16), dos, us)
        dqus = [
            (nn(do, e_ref[c, h]) + nn(da, ki_ref[half(c), cols(h)])) * jnp.exp(g_ref[half(c), cols(h)])
            for do, da, (c, h) in zip(dos, das, group)
        ]
        qs = [q_ref[half(c), cols(h)].astype(f32) for c, h in group]
        rqs = each(lambda q: inverse_norm(q), qs)
        qns = each(lambda q, rq: q * rq, qs, rqs)
        prods = each(lambda qn, dqu: qn * dqu, qns, dqus)
        dqs = each(
            lambda rq, dqu, qn, prod: (
                (rq * SCALE) * (dqu - qn * jnp.sum(prod, axis=-1, keepdims=True))
            ).astype(bf16),
            rqs, dqus, qns, prods,
        )
        for (c, h), dq, prod in zip(group, dqs, prods):
            dq_ref[half(c), cols(h)] = dq
            pq_ref[half(c), cols(h)] = (prod * SCALE).astype(bf16)


def kernel_c0(heads, g_ref, qd_ref, u_ref, do_ref, kk_ref):
    upper = triangle(True, f32)
    for group in units(heads, "c0"):
        us = [u_ref[half(c), cols(h)] for c, h in group]
        dos = [do_ref[half(c), cols(h)] for c, h in group]
        dats = each(lambda do, u: (nt(u, do) * upper).astype(bf16), dos, us)
        dkus = [
            nn(dat, qd_ref[half(c), cols(h)]) * jnp.exp(-g_ref[half(c), cols(h)])
            for dat, (c, h) in zip(dats, group)
        ]
        for (c, h), dku in zip(group, dkus):
            kk_ref[half(c), cols(h)] = dku.astype(bf16)


def kernel_c2(
    heads, resets, k_ref, g_ref, b_ref, wb_ref, kt_ref, n_ref, e_ref, vp_ref, u_ref, du_ref, dt_ref,
    pq_ref, kk_ref, g0, g1, g2, g3, dk_ref, dv_ref, dd_ref, db_ref, state,
):
    step = pl.program_id(0)
    turn = pl.num_programs(0) - 1 - step

    @pl.when(step == 0)
    def _():
        collect(inner(), state, (g0, g1, g2, g3))

    weights = twice(True)
    ones = jnp.ones((16, 128), bf16)
    grads = {}
    gbs = {}
    now = [state[h] for h in range(heads)]
    for c in reversed(range(STEP["c2"])):
        keep = (turn * STEP["c2"] + c != resets[0]).astype(f32)
        for h in range(heads):
            grads[c, h] = now[h]
            gbs[c, h] = now[h].astype(bf16)
        moved = split([
            nt(lanes(gbs[c, h], gbs[c, h + 1]), diag(n_ref[c, h], n_ref[c, h + 1])) for h in range(0, heads, 2)
        ])
        for h in range(heads):
            lam = jnp.exp(g_ref[64 * c + 63 : 64 * c + 64, cols(h)])
            now[h] = keep * (dt_ref[c, h].astype(f32) + lam * now[h] - moved[h])
    for h in range(heads):
        state[h] = now[h]
    for group in reversed(units(heads, "c2")):
        firsts = list(enumerate(group))[::2]
        both = [diag(gbs[c, h], gbs[c, h + 1]) for _, (c, h) in firsts]
        dus = split([
            (du_ref[half(c), wide(h)].astype(f32) + nt(kt_ref[half(c), wide(h)], x)).astype(bf16)
            for x, (_, (c, h)) in zip(both, firsts)
        ])
        dvs = [tn(wb_ref[c, :, half(h)], du) for du, (c, h) in zip(dus, group)]
        dvbs = each(lambda x: x.astype(bf16), dvs)
        gs = [g_ref[half(c), cols(h)] for c, h in group]
        ktts = split([nn(u_ref[half(c), wide(h)], x) for x, (_, (c, h)) in zip(both, firsts)])
        ktts = each(lambda x, g: x * jnp.exp(g[63:64, :] - g), ktts, gs)
        kdds = split([
            nn(lanes(dvbs[i], dvbs[i + 1]), diag(e_ref[c, h], e_ref[c, h + 1])) for i, (c, h) in firsts
        ])
        kdds = each(lambda x, g: x * jnp.exp(g), kdds, gs)
        ks = [k_ref[half(c), cols(h)].astype(f32) for c, h in group]
        rks = each(inverse_norm, ks)
        kus = each(lambda k, rk: k * rk, ks, rks)
        sums = [kk_ref[half(c), cols(h)].astype(f32) + ktt for ktt, (c, h) in zip(ktts, group)]
        dkus = each(lambda x, kdd: x - kdd, sums, kdds)
        dks = each(
            lambda rk, dku, ku: (rk * (dku - ku * jnp.sum(ku * dku, axis=-1, keepdims=True))).astype(bf16),
            rks, dkus, kus,
        )
        kutts = each(lambda ku, ktt: ku * ktt, kus, ktts)
        dgams = [
            pq_ref[half(c), cols(h)].astype(f32) - ku * (x + kdd) for ku, kdd, x, (c, h) in zip(kus, kdds, sums, group)
        ]
        dlasts = [
            jnp.sum(kutt, axis=0, keepdims=True)
            + jnp.exp(g[63:64, :]) * jnp.sum(grads[c, h] * e_ref[c, h].astype(f32), axis=0, keepdims=True)
            for kutt, g, (c, h) in zip(kutts, gs, group)
        ]
        dds = split([sum_rows(weights, lanes(dgams[i], dgams[i + 1])) for i, _ in firsts])
        dds = each(lambda x, dlast: x + dlast, dds, dlasts)
        dbs = [
            nt(ones, (dv * vp_ref[half(c), cols(h)].astype(f32)).astype(bf16))[0:1]
            for dv, (c, h) in zip(dvs, group)
        ]
        for (c, h), dvb, dk, dd, db in zip(group, dvbs, dks, dds, dbs):
            dv_ref[half(c), cols(h)] = dvb
            dk_ref[half(c), cols(h)] = dk
            dd_ref[half(c), cols(h)] = dd
            db_ref[h : h + 1, half(c)] = db / b_ref[h : h + 1, half(c)]


def identity_pair():
    row = lax.broadcasted_iota(jnp.int32, (256, 128), 0)
    col = lax.broadcasted_iota(jnp.int32, (256, 128), 1)
    return (row == col + 128).astype(bf16)


def after(pair, r):
    moved = nn(r, pair[128:256])
    return jnp.concatenate([moved[0:128] + pair[0:128].astype(f32), moved[128:256]], axis=0)


def kernel_f1(heads, p0, p1, p2, p3, total_ref, before_ref, slots):
    collect(inner(), slots, (p0, p1, p2, p3))
    before_ref[0] = identity_pair()
    r = slots[0]
    for z in range(1, RING):
        before_ref[z] = r
        r = after(slots[z], r).astype(bf16)
    total_ref[...] = r


def kernel_m(heads, slots, m_ref):
    row = lax.broadcasted_iota(jnp.int32, (128, 128), 0)
    col = lax.broadcasted_iota(jnp.int32, (128, 128), 1)
    m_ref[RING - 1] = (row == col).astype(bf16)
    m = slots[RING - 1, 128:256]
    m_ref[RING - 2] = m
    for z in reversed(range(1, RING - 1)):
        m = nn(slots[z, 128:256], m).astype(bf16)
        m_ref[z - 1] = m


def kernel_f2(heads, p0, p1, p2, p3, before, o0, o1, o2, o3, slots, states):
    me = outer()
    collect(me, slots, (p0, p1, p2, p3))
    s = jnp.where(me > 0, slots[0, 0:128].astype(f32), 0.0)
    for i in range(1, RING - 1):
        moved = nn(s.astype(bf16), slots[i, 128:256]) + slots[i, 0:128].astype(f32)
        s = jnp.where(i < me, moved, s)
    sb = s.astype(bf16)
    moved = [nn(sb, before[z, 128:256]) for z in range(RING)]
    for z in range(RING):
        states[z] = (moved[z] + before[z, 0:128].astype(f32)).astype(bf16)
    spread(inner(), states, (o0, o1, o2, o3))


def kernel_r1(heads, p0, p1, p2, p3, before, total_ref, slots):
    collect(inner(), slots, (p0, p1, p2, p3))
    parts = [nt(slots[z], before[z, 128:256]) for z in range(1, RING)]
    total_ref[...] = (slots[0].astype(f32) + sum(parts)).astype(bf16)


def kernel_r3(heads, slots, zslots, later_ref):
    later_ref[RING - 1] = jnp.zeros((128, 128), bf16)
    g = slots[RING - 1]
    later_ref[RING - 2] = g
    for z in reversed(range(1, RING - 1)):
        g = (nt(g, zslots[z, 128:256]) + slots[z].astype(f32)).astype(bf16)
        later_ref[z - 1] = g


def kernel_r2(heads, p0, p1, p2, p3, later, later_m, yslots, o0, o1, o2, o3, slots, grads):
    me = outer()
    collect(me, slots, (p0, p1, p2, p3))
    g = jnp.where(me < RING - 1, slots[RING - 1].astype(f32), 0.0)
    for i in reversed(range(1, RING - 1)):
        moved = nt(g.astype(bf16), yslots[i, 128:256]) + slots[i].astype(f32)
        g = jnp.where(i > me, moved, g)
    gb = g.astype(bf16)
    moved = [nt(gb, later_m[z]) for z in range(RING)]
    for z in range(RING):
        grads[z] = (moved[z] + later[z].astype(f32)).astype(bf16)
    spread(inner(), grads, (o0, o1, o2, o3))


def permute(x, distance, outer):
    size = lax.axis_size("seq")
    if outer:
        pairs = [(i, (i + RING * distance) % size) for i in range(size)]
    else:
        pairs = [(i, i // RING * RING + (i + distance) % RING) for i in range(size)]
    return lax.ppermute(x, "seq", pairs)


def three(x, outer):
    arrays = [x] * RING if outer else x
    return [arrays[0]] + [permute(arrays[distance], distance, outer) for distance in (1, 2, 3)]


LIMIT = dict(a1=54, a2=54, b=53, c0=54, c1=54, c2=53)
SMEM = pl.BlockSpec(memory_space=pltpu.SMEM)
VMEM = pl.BlockSpec(memory_space=pltpu.VMEM)


def shape(dims, dtype):
    return jax.ShapeDtypeStruct(dims, dtype)


def call(body, name, heads, in_specs, out_specs, out_shape, scratch, grid, flops, *args, into=()):
    total = sum(a.size * a.dtype.itemsize for a in args)
    total += sum(o.size * o.dtype.itemsize for o in out_shape)
    return pl.pallas_call(
        functools.partial(body, heads),
        out_shape=out_shape,
        grid=grid,
        in_specs=in_specs,
        out_specs=out_specs,
        scratch_shapes=scratch,
        input_output_aliases={len(args) + i: i for i in range(len(into))},
        compiler_params=pltpu.CompilerParams(
            vmem_limit_bytes=LIMIT.get(name, 8) * 2**20,
            **({"dimension_semantics": ("arbitrary",)} if grid else {}),
        ),
        cost_estimate=pl.CostEstimate(flops=flops, bytes_accessed=total, transcendentals=0),
        name=name,
    )(*args, *into)


def per_device(
    queries, keys, values, decay, beta, wy_inverse, out_gate, norm_gain, out_proj, grad_out, resets
):
    tokens = queries.shape[0]
    heads = beta.shape[0]
    count = tokens // GROUP
    width = heads * 128
    gathered = lax.all_gather(grad_out.T, "head", axis=0, tiled=True)
    model = out_proj.shape[1]

    def specs(name, back=False):
        step = STEP[name]
        steps = count // step
        at = (lambda i: steps - 1 - i) if back else (lambda i: i)
        return dict(
            grid=(steps,),
            tok=pl.BlockSpec((step * GROUP, width), lambda i: (at(i), 0)),
            beta=pl.BlockSpec((heads, step * GROUP), lambda i: (0, at(i))),
            wy=pl.BlockSpec((step, GROUP, heads * GROUP), lambda i: (at(i), 0, 0)),
            state=pl.BlockSpec((step, heads, 128, 128), lambda i: (at(i), 0, 0, 0)),
            pair=pl.BlockSpec((step, heads, 256, 128), lambda i: (at(i), 0, 0, 0)),
            whole=pl.BlockSpec((128, 128), lambda i: (0, 0)),
            whole2=pl.BlockSpec((256, 128), lambda i: (0, 0)),
            parts=pl.BlockSpec((model, step * GROUP), lambda i: (0, at(i))),
            proj=pl.BlockSpec((width, model), lambda i: (0, 0)),
            gain=pl.BlockSpec((1, 128), lambda i: (0, 0)),
        )

    tok_b = shape((tokens, width), bf16)
    tok_f = shape((tokens, width), f32)
    small_b = shape((count, GROUP, heads * GROUP), bf16)
    state_b = shape((count, heads, 128, 128), bf16)
    pair_b = shape((count, heads, 256, 128), bf16)
    one_b = shape((128, 128), bf16)
    two_b = shape((256, 128), bf16)
    ones_b = shape((RING, 128, 128), bf16)
    twos_b = shape((RING, 256, 128), bf16)
    unit = count * heads * 2 * 64 * 128 * 128

    s = specs("a1")
    gamma, wb, kd, kt, y, n, pre, *mb = call(
        kernel_a1, "a1", heads,
        [SMEM, s["tok"], s["tok"], s["tok"], s["beta"], s["wy"]],
        [s["tok"], s["wy"], s["tok"], s["tok"], s["tok"], s["state"], s["pair"]] + [s["whole2"]] * 4,
        [tok_f, small_b, tok_b, tok_b, tok_b, state_b, pair_b] + [two_b] * 4,
        [pltpu.VMEM((heads, 256, 128), f32)], s["grid"], 8 * unit,
        resets, keys, values, decay, beta, wy_inverse,
    )
    zs = three(mb, False)
    s = specs("a2")
    qd, ki, a, at = call(
        kernel_a2, "a2", heads,
        [s["tok"], s["tok"], s["tok"]],
        [s["tok"], s["tok"], s["wy"], s["wy"]],
        [tok_b, tok_b, small_b, small_b],
        [], s["grid"], 2 * unit, queries, keys, gamma,
    )
    zs, qd = lax.optimization_barrier((zs, qd))
    group, before, zslots = call(
        kernel_f1, "f1", heads, [VMEM] * 4, [VMEM] * 3, [two_b, twos_b, twos_b], [], (),
        unit // 8, *zs,
    )
    ys = three(group, True)
    (later_m,) = call(kernel_m, "m", heads, [VMEM], [VMEM], [ones_b], [], (), unit // 16, zslots)
    ys, later_m = lax.optimization_barrier((ys, later_m))
    *states, yslots = call(
        kernel_f2, "f2", heads, [VMEM] * 5, [VMEM] * 5, [one_b] * 4 + [twos_b],
        [pltpu.VMEM((RING, 128, 128), bf16)], (), unit // 8, *ys, before,
    )
    state_in = three(states, False)
    s = specs("b")
    e, vp, u, do, du, dt, dgate, *r = call(
        kernel_b, "b", heads,
        [s["tok"], s["tok"], s["tok"], s["tok"], s["wy"], s["wy"], s["wy"], s["pair"], s["tok"], s["parts"], s["proj"], s["gain"]] + [s["whole"]] * 4,
        [s["state"], s["tok"], s["tok"], s["tok"], s["tok"], s["state"], s["tok"]] + [s["whole"]] * 4,
        [state_b, tok_b, tok_b, tok_b, tok_b, state_b, tok_b] + [one_b] * 4,
        [pltpu.VMEM((heads, 128, 128), f32), pltpu.VMEM((heads, 128, 128), bf16)], s["grid"], 12 * unit,
        values, kd, qd, y, wb, a, at, pre, out_gate, gathered, out_proj, norm_gain.reshape(1, 128), *state_in,
    )
    zr = three(r, False)
    s = specs("c0")
    (kk,) = call(
        kernel_c0, "c0", heads, [s["tok"]] * 4, [s["tok"]], [tok_b], [], s["grid"], 2 * unit, gamma, qd, u, do,
    )
    zr, kk = lax.optimization_barrier((zr, kk))
    rgroup, rslots = call(
        kernel_r1, "r1", heads, [VMEM] * 5, [VMEM] * 2, [one_b, ones_b], [], (),
        unit // 16, *zr, before,
    )
    yr = three(rgroup, True)
    (later,) = call(kernel_r3, "r3", heads, [VMEM] * 2, [VMEM], [ones_b], [], (), unit // 16, rslots, zslots)

    def gradient_q(part, into):
        steps = count // STEP["c1"] // 2
        tok = pl.BlockSpec((STEP["c1"] * GROUP, width), lambda i: (i + part * steps, 0))
        state = pl.BlockSpec((STEP["c1"], heads, 128, 128), lambda i: (i + part * steps, 0, 0, 0))
        return call(
            kernel_c1, "c1", heads,
            [tok] * 5 + [state] + [pl.BlockSpec(memory_space=pl.ANY)] * len(into),
            [tok, tok], [tok_b, tok_b],
            [], (steps,), 2 * unit, queries, gamma, ki, u, do, e, into=into,
        )

    dq, pq = gradient_q(0, ())
    yr, later, pq = lax.optimization_barrier((yr, later, pq))
    *grads, _ = call(
        kernel_r2, "r2", heads, [VMEM] * 7, [VMEM] * 5, [one_b] * 4 + [ones_b],
        [pltpu.VMEM((RING, 128, 128), bf16)], (), unit // 16, *yr, later, later_m, yslots,
    )
    grad_in = three(grads, False)
    dq, pq = gradient_q(1, (dq, pq))
    grad_in, pq = lax.optimization_barrier((grad_in, pq))
    s = specs("c2", True)
    dk, dv, dd, db = call(
        kernel_c2, "c2", heads,
        [SMEM, s["tok"], s["tok"], s["beta"], s["wy"], s["tok"], s["state"], s["state"], s["tok"], s["tok"], s["tok"], s["state"], s["tok"], s["tok"]] + [s["whole"]] * 4,
        [s["tok"], s["tok"], s["tok"], s["beta"]],
        [tok_b, tok_b, tok_f, shape((heads, tokens), f32)],
        [pltpu.VMEM((heads, 128, 128), f32)], s["grid"], 10 * unit,
        resets, keys, gamma, beta, wb, kt, n, e, vp, u, du, dt, pq, kk, *grad_in,
    )
    return dq, dk, dv, dd, db, dgate


def solution(mesh):
    return jax.shard_map(
        per_device,
        mesh=mesh,
        in_specs=(
            P("seq", "head"),
            P("seq", "head"),
            P("seq", "head"),
            P("seq", "head"),
            P("head", "seq"),
            P("seq", None, "head"),
            P("seq", "head"),
            P(),
            P("head", None),
            P("seq", "head"),
            P("seq"),
        ),
        out_specs=(
            P("seq", "head"),
            P("seq", "head"),
            P("seq", "head"),
            P("seq", "head"),
            P("head", "seq"),
            P("seq", "head"),
        ),
        check_vma=False,
    )
```
